32 devices in a mesh: row: 8 (over y, x, core), col: 4 (over z).
Axes of the slice: x: 2, y: 2, z: 4, core: 2. Of those that a mesh axis runs over, the one named last changes fastest.
Arguments:
- slab: float32 [4096, 10240], P('row', 'col'), may hold values from -6 to 6
- leaf_y: float32 [4096, 256], P('row', 'col'), may hold values from -0.25 to 0.25
- leaf_t: float32 [2048, 256], P('row', 'col'), may hold values from -0.2 to 2.3, as said below
- tree_y: float32 [3, 2048, 256], P(None, 'row'), may hold values from -0.25 to 0.25
- tree_t: float32 [3, 2048, 256], P(None, 'row'), may hold values from -0.2 to 2.3, as said below
Outputs:
- result: float32 [4096, 10240], P('row', 'col')
The draws below stay inside these ranges and needn't reach their ends.
Inputs may be any that keep to these rules, and one draw needn't show every extreme that they name: `leaf_t`: each 256 x 256 block is upper triangular, with diagonal entries between 1.7 and 2.3 and off-diagonal entries of magnitude at most 0.2. `tree_t`: each 256 x 256 block is upper triangular, with diagonal entries between 1.7 and 2.3 and off-diagonal entries of magnitude at most 0.2; blocks of a section s that do not belong to a node's lower member are not used.
All inputs are finite; a program needn't handle non-finite values.
Results may differ from the reference program's by a relative error of at most 0.0002.
Values sent between devices are 32-bit elements; how exact they have to be, the bound alone decides.
A program may use at most 64 MiB of HBM per device.

```python
import math
import jax
import jax.numpy as jnp
from jax import lax

B = 256
NCOL = 10240
ROWS_DEV = 512
SECTIONS = 3
M = 4096
N_ROW = 8


def triangle(key, count, low_end, high_end, spread):
    first, second = jax.random.split(jax.random.fold_in(key, 17))
    diag_vals = jax.random.uniform(first, (count * B, B), jnp.float32, low_end, high_end)
    off_vals = jnp.clip(jax.random.normal(second, (count * B, B), jnp.float32) * spread / math.sqrt(B), -0.2, 0.2)
    row_pos = jnp.arange(count * B) % B
    col_pos = jnp.arange(B)
    upper = col_pos[None, :] > row_pos[:, None]
    same = col_pos[None, :] == row_pos[:, None]
    return jnp.where(same, diag_vals, jnp.where(upper, off_vals, 0.0))


def draw_leaf_t(key, part):
    return triangle(key, N_ROW, 1.8, 2.2, 0.4)


def draw_tree_t(key, part):
    values = triangle(key, SECTIONS * N_ROW, 1.8, 2.2, 0.4)
    return values.reshape(SECTIONS, N_ROW * B, B)


def shard_levels(own_key, shape, shards, least, largest):
    level, own = 1.0, jax.random.fold_in(own_key, 6)
    for position, shards_of in shards:
        draws = jnp.exp(jax.random.uniform(jax.random.fold_in(own, position), (shards_of,), jnp.float32, least / len(shards), largest / len(shards)))
        level = level * jnp.repeat(draws, shape[position] // shards_of).reshape([-1 if axis == position else 1 for axis in range(len(shape))])
    return level


def noise(rng, extent, width, bound, pieces=(), dtype=jnp.bfloat16):
    values = jax.random.normal(rng, extent, jnp.float32) * width
    if len(pieces) > 0:
        values = shard_levels(rng, extent, pieces, -0.22, 0.18) * values
    return jnp.clip(values, min=-bound, max=bound).astype(dtype)


def setup_inputs(seed: int = 0) -> dict:
    splits = jax.random.split(jax.random.key(seed), 6)
    return {
        "slab": noise(splits[0], (M, NCOL), 1.0, 6.0, ((0, 8), (1, 4)), jnp.float32),
        "leaf_y": noise(splits[1], (M, B), ROWS_DEV ** -0.5, 0.25, ((0, 8), (1, 4)), jnp.float32),
        "leaf_t": draw_leaf_t(jax.random.fold_in(splits[5], 71), 0),
        "tree_y": noise(splits[3], (SECTIONS, N_ROW * B, B), (2 * B) ** -0.5, 0.25, ((1, 8),), jnp.float32),
        "tree_t": draw_tree_t(jax.random.fold_in(splits[5], 71), 0),
    }


def contract(left, right):
    return lax.dot_general(left, right, (((0,), (0,)), ((), ())), precision=lax.Precision.HIGHEST, preferred_element_type=jnp.float32)


def reflect(vectors, factor, block):
    coeffs = contract(vectors, block)
    scaled = contract(factor, coeffs)
    return block - jnp.dot(vectors, scaled, precision=lax.Precision.HIGHEST, preferred_element_type=jnp.float32)


def reference(slab, leaf_y, leaf_t, tree_y, tree_t):
    blocks = slab.reshape(N_ROW, ROWS_DEV, NCOL)
    vectors = leaf_y.reshape(N_ROW, ROWS_DEV, B)
    factors = leaf_t.reshape(N_ROW, B, B)
    updated = lax.map(lambda trio: reflect(trio[0], trio[1], trio[2]), (vectors, factors, blocks))
    heads = updated[:, :B, :]
    for section in range(SECTIONS):
        stride = 2 ** section
        groups = N_ROW // (2 * stride)
        grouped = heads.reshape(groups, 2, stride, B, NCOL)
        first_rows = grouped[:, 0, 0]
        second_rows = grouped[:, 1, 0]
        node_y = tree_y[section].reshape(groups, 2, stride, B, B)
        first_y = node_y[:, 0, 0]
        second_y = node_y[:, 1, 0]
        node_t = tree_t[section].reshape(groups, 2, stride, B, B)[:, 0, 0]
        coeffs = jnp.einsum("grb,grc->gbc", first_y, first_rows, precision=lax.Precision.HIGHEST)
        coeffs = coeffs + jnp.einsum("grb,grc->gbc", second_y, second_rows, precision=lax.Precision.HIGHEST)
        scaled = jnp.einsum("gbk,gbc->gkc", node_t, coeffs, precision=lax.Precision.HIGHEST)
        first_rows = first_rows - jnp.einsum("grk,gkc->grc", first_y, scaled, precision=lax.Precision.HIGHEST)
        second_rows = second_rows - jnp.einsum("grk,gkc->grc", second_y, scaled, precision=lax.Precision.HIGHEST)
        grouped = grouped.at[:, 0, 0].set(first_rows).at[:, 1, 0].set(second_rows)
        heads = grouped.reshape(N_ROW, B, NCOL)
    result = jnp.concatenate([heads, updated[:, B:, :]], axis=1)
    return result.reshape(M, NCOL)
```

```python
import functools

import jax
import jax.numpy as jnp
from jax import lax
from jax.experimental import pallas as pl
from jax.experimental.pallas import tpu as pltpu
from jax.sharding import PartitionSpec as P

MESH = pl.DeviceIdType.MESH


def halves(x):
    high = x.astype(jnp.bfloat16)
    return high, (x - high.astype(jnp.float32)).astype(jnp.bfloat16)


def dot3(left, right, dims=((1,), (0,))):
    def one(a, b):
        return lax.dot_general(a, b, (dims, ((), ())), preferred_element_type=jnp.float32)

    return one(left[0], right[0]) + (one(left[0], right[1]) + one(left[1], right[0]))


def kernel(
    sizes,
    slab_hbm, leaf_y, leaf_t, tree_y_hbm, tree_t_hbm,
    out_hbm,
    slab, head, part_out, part_in, tree_y, tree_t,
    gather_y, gather_t, y_t, v, node_y_t, node_v,
    slab_sem, out_sem, part_send, part_recv, y_sem,
    t_local, t_send, t_recv, gather_send, gather_recv,
):
    peers, sections, chunks, width, chunk_cols, shard = sizes
    row, col = lax.axis_index("row"), lax.axis_index("col")
    partner = [jnp.bitwise_xor(row, 1 << s) for s in range(sections)]
    active = [lax.rem(row, 1 << s) == 0 for s in range(sections)]
    lower = [lax.rem(row, 2 << s) == 0 for s in range(sections)]

    def columns(c):
        return pl.ds(pl.multiple_of(c * chunk_cols, chunk_cols), chunk_cols)

    def slab_copy(c):
        return pltpu.make_async_copy(slab_hbm.at[:, columns(c)], slab.at[c], slab_sem.at[c])

    def tail_copy(c):
        return pltpu.make_async_copy(
            slab.at[c, pl.ds(width, width)], out_hbm.at[pl.ds(width, width), columns(c)], out_sem.at[1, c]
        )

    def head_copy(c):
        return pltpu.make_async_copy(
            head.at[c], out_hbm.at[pl.ds(0, width), columns(c)], out_sem.at[0, c]
        )

    def part_copy(s, c):
        return pltpu.make_async_remote_copy(
            src_ref=part_out.at[s, c], dst_ref=part_in.at[s, c],
            send_sem=part_send.at[s, c], recv_sem=part_recv.at[s, c],
            device_id={"row": partner[s]}, device_id_type=MESH,
        )

    def factor_copy(s):
        return pltpu.make_async_remote_copy(
            src_ref=tree_t_hbm.at[s], dst_ref=tree_t.at[s],
            send_sem=t_send.at[s], recv_sem=t_recv.at[s],
            device_id={"row": partner[s]}, device_id_type=MESH,
        )

    def factor_local(s):
        return pltpu.make_async_copy(tree_t_hbm.at[s], tree_t.at[s], t_local.at[s])

    mine = pl.ds(pl.multiple_of(col * shard, shard), shard)

    def gather_copy(which, d):
        buffer = (gather_y, gather_t)[which]
        return pltpu.make_async_remote_copy(
            src_ref=buffer.at[mine], dst_ref=buffer.at[mine],
            send_sem=gather_send.at[which, d], recv_sem=gather_recv.at[which, d],
            device_id={"col": lax.rem(col + d, peers)}, device_id_type=MESH,
        )

    barrier = pltpu.get_barrier_semaphore()
    for d in range(1, peers):
        pl.semaphore_signal(
            barrier, inc=1, device_id={"col": lax.rem(col + d, peers)}, device_id_type=MESH
        )
    for s in range(sections):
        pl.semaphore_signal(barrier, inc=1, device_id={"row": partner[s]}, device_id_type=MESH)

    y_copy = pltpu.make_async_copy(tree_y_hbm, tree_y, y_sem)
    y_copy.start()
    for s in range(sections):
        pl.when(lower[s])(lambda s=s: factor_local(s).start())
    for c in range(chunks):
        slab_copy(c).start()
    gather_y[mine, :] = leaf_y[...].T
    gather_t[mine, :] = leaf_t[...].T

    pl.semaphore_wait(barrier, peers - 1 + sections)
    for which in range(2):
        for d in range(1, peers):
            gather_copy(which, d).start()
    for s in range(sections):
        pl.when(lower[s])(lambda s=s: factor_copy(s).start())

    y_copy.wait()
    for s in range(sections):
        pl.when(lower[s])(lambda s=s: factor_local(s).wait())
        pl.when(jnp.logical_and(active[s], jnp.logical_not(lower[s])))(
            lambda s=s: factor_copy(s).wait_recv()
        )

        @pl.when(active[s])
        def _(s=s):
            vectors = tree_y[s]
            node_y_t[s, 0], node_y_t[s, 1] = halves(vectors.T)
            product = dot3(halves(vectors), halves(tree_t[s]), ((1,), (1,)))
            node_v[s, 0], node_v[s, 1] = halves(product)

    for which in range(2):
        for d in range(1, peers):
            gather_copy(which, d).wait_recv()
    all_y_t = gather_y[...]
    y_t[0], y_t[1] = halves(all_y_t)
    product = dot3(halves(all_y_t.T), halves(gather_t[...]))
    v[0], v[1] = halves(product)

    def send_part(s, c, rows):
        part_out[s, c] = dot3((node_y_t[s, 0], node_y_t[s, 1]), halves(rows))
        part_copy(s, c).start()

    def leaf(c):
        slab_copy(c).wait()
        block = slab[c]
        coeffs = dot3((y_t[0], y_t[1]), halves(block))
        updated = block - dot3((v[0], v[1]), halves(coeffs))
        rows = updated[:width]
        head[c] = rows
        slab[c, width:, :] = updated[width:]
        tail_copy(c).start()
        send_part(0, c, rows)

    def node(s, c):
        part_copy(s, c).wait_recv()
        coeffs = part_out[s, c] + part_in[s, c]
        rows = head[c] - dot3((node_v[s, 0], node_v[s, 1]), halves(coeffs))
        head[c] = rows
        if s + 1 < sections:
            pl.when(active[s + 1])(lambda: send_part(s + 1, c, rows))
            pl.when(jnp.logical_not(active[s + 1]))(lambda: head_copy(c).start())
        else:
            head_copy(c).start()

    lag = [1 + 2 * s for s in range(sections)]

    def step(t, carry):
        pl.when(t < chunks)(lambda: leaf(t))
        for s in range(sections):
            c = t - lag[s]
            inside = jnp.logical_and(c >= 0, c < chunks)
            pl.when(jnp.logical_and(active[s], inside))(lambda s=s, c=c: node(s, c))
        return carry

    lax.fori_loop(0, chunks + lag[-1], step, 0)

    def finish(c, carry):
        tail_copy(c).wait()
        head_copy(c).wait()
        for s in range(sections):
            pl.when(active[s])(lambda s=s: part_copy(s, c).wait_send())
        return carry

    lax.fori_loop(0, chunks, finish, 0)
    for which in range(2):
        for d in range(1, peers):
            gather_copy(which, d).wait_send()
    for s in range(sections):
        pl.when(lower[s])(lambda s=s: factor_copy(s).wait_send())


def shards(slab, leaf_y, leaf_t, tree_y, tree_t):
    peers = lax.axis_size("col")
    rows, cols = slab.shape
    sections, width, _ = tree_y.shape
    shard = leaf_y.shape[1]
    chunk_cols = next(size for size in (256, 128) if cols % size == 0)
    chunks = cols // chunk_cols
    f32, bf16 = jnp.float32, jnp.bfloat16
    sizes = (peers, sections, chunks, width, chunk_cols, shard)
    any_space = pl.BlockSpec(memory_space=pl.ANY)
    vmem = pl.BlockSpec(memory_space=pltpu.VMEM)
    dma = pltpu.SemaphoreType.DMA
    flops = 4 * cols * width * (rows + sections * width) * 3
    return pl.pallas_call(
        functools.partial(kernel, sizes),
        out_shape=jax.ShapeDtypeStruct(slab.shape, f32),
        in_specs=[any_space, vmem, vmem, any_space, any_space],
        out_specs=any_space,
        scratch_shapes=[
            pltpu.VMEM((chunks, rows, chunk_cols), f32),
            pltpu.VMEM((chunks, width, chunk_cols), f32),
            pltpu.VMEM((sections, chunks, width, chunk_cols), f32),
            pltpu.VMEM((sections, chunks, width, chunk_cols), f32),
            pltpu.VMEM(tree_y.shape, f32),
            pltpu.VMEM(tree_t.shape, f32),
            pltpu.VMEM((width, rows), f32),
            pltpu.VMEM((width, width), f32),
            pltpu.VMEM((2, width, rows), bf16),
            pltpu.VMEM((2, rows, width), bf16),
            pltpu.VMEM((sections, 2, width, width), bf16),
            pltpu.VMEM((sections, 2, width, width), bf16),
            dma((chunks,)),
            dma((2, chunks)),
            dma((sections, chunks)),
            dma((sections, chunks)),
            dma,
            dma((sections,)),
            dma((sections,)),
            dma((sections,)),
            dma((2, peers)),
            dma((2, peers)),
        ],
        compiler_params=pltpu.CompilerParams(
            collective_id=0, has_side_effects=True, vmem_limit_bytes=52 * 2**20
        ),
        cost_estimate=pl.CostEstimate(
            flops=flops, bytes_accessed=8 * rows * cols, transcendentals=0
        ),
    )(slab, leaf_y, leaf_t, tree_y, tree_t)


def solution(mesh):
    in_specs = (
        P("row", "col"),
        P("row", "col"),
        P("row", "col"),
        P(None, "row", None),
        P(None, "row", None),
    )
    out_specs = P("row", "col")
    return jax.shard_map(shards, mesh=mesh, in_specs=in_specs, out_specs=out_specs, check_vma=False)
```

```python
import functools

import jax
import jax.numpy as jnp
from jax import lax
from jax.experimental import pallas as pl
from jax.experimental.pallas import tpu as pltpu
from jax.sharding import PartitionSpec as P

MESH = pl.DeviceIdType.MESH


def halves(x):
    high = x.astype(jnp.bfloat16)
    return high, (x - high.astype(jnp.float32)).astype(jnp.bfloat16)


def dot3(left, right, dims=((1,), (0,))):
    def one(a, b):
        return lax.dot_general(a, b, (dims, ((), ())), preferred_element_type=jnp.float32)

    return one(left[0], right[0]) + (one(left[0], right[1]) + one(left[1], right[0]))


def kernel(
    sizes,
    slab_hbm, leaf_y, leaf_t, tree_y_hbm, tree_t_hbm,
    out_hbm,
    slab, head, part_out, part_in, tree_y, tree_t,
    gather_y, gather_t, y_t, v, v_sum, node_y_t, node_v,
    slab_sem, out_sem, part_send, part_recv, y_sem,
    t_local, t_send, t_recv, gather_send, gather_recv,
):
    peers, sections, chunks, width, chunk_cols, shard = sizes
    row, col = lax.axis_index("row"), lax.axis_index("col")
    partner = [jnp.bitwise_xor(row, 1 << s) for s in range(sections)]
    active = [lax.rem(row, 1 << s) == 0 for s in range(sections)]
    lower = [lax.rem(row, 2 << s) == 0 for s in range(sections)]

    def columns(c):
        return pl.ds(pl.multiple_of(c * chunk_cols, chunk_cols), chunk_cols)

    def slab_copy(c):
        return pltpu.make_async_copy(slab_hbm.at[:, columns(c)], slab.at[c], slab_sem.at[c])

    def tail_copy(c):
        return pltpu.make_async_copy(
            slab.at[c, pl.ds(width, width)], out_hbm.at[pl.ds(width, width), columns(c)], out_sem.at[1, c]
        )

    def head_copy(c):
        return pltpu.make_async_copy(
            head.at[c], out_hbm.at[pl.ds(0, width), columns(c)], out_sem.at[0, c]
        )

    def part_copy(s, c):
        return pltpu.make_async_remote_copy(
            src_ref=part_out.at[s, c], dst_ref=part_in.at[s, c],
            send_sem=part_send.at[s, c], recv_sem=part_recv.at[s, c],
            device_id={"row": partner[s]}, device_id_type=MESH,
        )

    def factor_copy(s):
        return pltpu.make_async_remote_copy(
            src_ref=tree_t_hbm.at[s], dst_ref=tree_t.at[s],
            send_sem=t_send.at[s], recv_sem=t_recv.at[s],
            device_id={"row": partner[s]}, device_id_type=MESH,
        )

    def factor_local(s):
        return pltpu.make_async_copy(tree_t_hbm.at[s], tree_t.at[s], t_local.at[s])

    short = peers % 2 == 0 and width % 256 == 0

    def of(owner):
        return pl.ds(pl.multiple_of(owner * shard, shard), shard)

    def y_shard(d):
        return pltpu.make_async_remote_copy(
            src_ref=gather_y.at[of(col)], dst_ref=gather_y.at[of(col)],
            send_sem=gather_send.at[0, d], recv_sem=gather_recv.at[0, d],
            device_id={"col": lax.rem(col + d, peers)}, device_id_type=MESH,
        )

    def t_shard(d, kept):
        block = gather_t.at[of(col), pl.ds(0, kept)]
        return pltpu.make_async_remote_copy(
            src_ref=block, dst_ref=block,
            send_sem=gather_send.at[1, d], recv_sem=gather_recv.at[1, d],
            device_id={"col": lax.rem(col + d, peers)}, device_id_type=MESH,
        )

    def by_shard(owner, act):
        if short:
            early = 2 * owner < peers
            pl.when(early)(lambda: act(width // 2))
            pl.when(jnp.logical_not(early))(lambda: act(width))
        else:
            act(width)

    barrier = pltpu.get_barrier_semaphore()
    for d in range(1, peers):
        pl.semaphore_signal(
            barrier, inc=1, device_id={"col": lax.rem(col + d, peers)}, device_id_type=MESH
        )
    for s in range(sections):
        pl.semaphore_signal(barrier, inc=1, device_id={"row": partner[s]}, device_id_type=MESH)

    y_copy = pltpu.make_async_copy(tree_y_hbm, tree_y, y_sem)
    y_copy.start()
    for s in range(sections):
        pl.when(lower[s])(lambda s=s: factor_local(s).start())
    for c in range(chunks):
        slab_copy(c).start()
    if short:
        gather_t[pl.ds(0, width // 2), pl.ds(width // 2, width // 2)] = jnp.zeros(
            (width // 2, width // 2), jnp.float32
        )
    gather_y[of(col), :] = leaf_y[...]
    gather_t[of(col), :] = leaf_t[...]

    pl.semaphore_wait(barrier, peers - 1 + sections)
    for d in range(1, peers):
        y_shard(d).start()
    for d in range(1, peers):
        by_shard(col, lambda kept, d=d: t_shard(d, kept).start())
    for s in range(sections):
        pl.when(lower[s])(lambda s=s: factor_copy(s).start())

    y_copy.wait()
    for s in range(sections):
        pl.when(lower[s])(lambda s=s: factor_local(s).wait())
        pl.when(jnp.logical_and(active[s], jnp.logical_not(lower[s])))(
            lambda s=s: factor_copy(s).wait_recv()
        )

        @pl.when(active[s])
        def _(s=s):
            vectors = tree_y[s]
            node_y_t[s, 0], node_y_t[s, 1] = halves(vectors.T)
            product = dot3(halves(vectors), halves(tree_t[s]), ((1,), (1,)))
            node_v[s, 0], node_v[s, 1] = halves(product)

    for d in range(peers):
        owner = lax.rem(col - d + peers, peers)
        if d:
            y_shard(d).wait_recv()
        vectors = gather_y[of(owner), :]
        y_t[0, of(owner), :], y_t[1, of(owner), :] = halves(vectors)
        turned = halves(vectors.T)
        if d:
            by_shard(owner, lambda kept, d=d: t_shard(d, kept).wait_recv())
        term = dot3(turned, halves(gather_t[of(owner), :]))
        total = v_sum[...] + term if d else term
        if d < peers - 1:
            v_sum[...] = total
        else:
            v[0], v[1] = halves(total)

    def send_part(s, c, rows):
        part_out[s, c] = dot3((node_y_t[s, 0], node_y_t[s, 1]), halves(rows))
        part_copy(s, c).start()

    def leaf(c):
        slab_copy(c).wait()
        block = slab[c]
        coeffs = dot3((y_t[0], y_t[1]), halves(block))
        updated = block - dot3((v[0], v[1]), halves(coeffs))
        rows = updated[:width]
        head[c] = rows
        slab[c, width:, :] = updated[width:]
        tail_copy(c).start()
        send_part(0, c, rows)

    def node(s, c):
        part_copy(s, c).wait_recv()
        coeffs = part_out[s, c] + part_in[s, c]
        rows = head[c] - dot3((node_v[s, 0], node_v[s, 1]), halves(coeffs))
        head[c] = rows
        if s + 1 < sections:
            pl.when(active[s + 1])(lambda: send_part(s + 1, c, rows))
            pl.when(jnp.logical_not(active[s + 1]))(lambda: head_copy(c).start())
        else:
            head_copy(c).start()

    lag = [1 + (s and 1 + 2 * s) for s in range(sections)]

    def step(t, carry):
        pl.when(t < chunks)(lambda: leaf(t))
        for s in range(sections):
            c = t - lag[s]
            inside = jnp.logical_and(c >= 0, c < chunks)
            pl.when(jnp.logical_and(active[s], inside))(lambda s=s, c=c: node(s, c))
        return carry

    lax.fori_loop(0, chunks + lag[-1], step, 0)

    def finish(c, carry):
        tail_copy(c).wait()
        head_copy(c).wait()
        for s in range(sections):
            pl.when(active[s])(lambda s=s: part_copy(s, c).wait_send())
        return carry

    lax.fori_loop(0, chunks, finish, 0)
    for d in range(1, peers):
        y_shard(d).wait_send()
        by_shard(col, lambda kept, d=d: t_shard(d, kept).wait_send())
    for s in range(sections):
        pl.when(lower[s])(lambda s=s: factor_copy(s).wait_send())


def place(bands, band, mixed_hbm, out_hbm, held, in_sem, out_sem):
    def copy_in(b):
        return pltpu.make_async_copy(mixed_hbm.at[pl.ds(b * band, band)], held.at[b], in_sem.at[b])

    def copy_out(b):
        return pltpu.make_async_copy(held.at[b], out_hbm.at[pl.ds(b * band, band)], out_sem.at[b])

    for b in range(bands):
        copy_in(b).start()
    for b in range(bands):
        copy_in(b).wait()
        copy_out(b).start()
    for b in range(bands):
        copy_out(b).wait()


def shards(slab, leaf_y, leaf_t, tree_y, tree_t):
    peers = lax.axis_size("col")
    rows, cols = slab.shape
    sections, width, _ = tree_y.shape
    shard = leaf_y.shape[1]
    chunk_cols = next(size for size in (256, 128) if cols % size == 0)
    chunks = cols // chunk_cols
    f32, bf16 = jnp.float32, jnp.bfloat16
    sizes = (peers, sections, chunks, width, chunk_cols, shard)
    vmem = pl.BlockSpec(memory_space=pltpu.VMEM)
    dma = pltpu.SemaphoreType.DMA
    flops = 4 * cols * width * (rows + sections * width) * 3
    hbm = pl.BlockSpec(memory_space=pltpu.HBM)
    mixed = pl.pallas_call(
        functools.partial(kernel, sizes),
        out_shape=jax.ShapeDtypeStruct(slab.shape, f32),
        in_specs=[hbm, vmem, vmem, hbm, hbm],
        out_specs=hbm,
        scratch_shapes=[
            pltpu.VMEM((chunks, rows, chunk_cols), f32),
            pltpu.VMEM((chunks, width, chunk_cols), f32),
            pltpu.VMEM((sections, chunks, width, chunk_cols), f32),
            pltpu.VMEM((sections, chunks, width, chunk_cols), f32),
            pltpu.VMEM(tree_y.shape, f32),
            pltpu.VMEM(tree_t.shape, f32),
            pltpu.VMEM((width, rows), f32),
            pltpu.VMEM((width, width), f32),
            pltpu.VMEM((2, width, rows), bf16),
            pltpu.VMEM((2, rows, width), bf16),
            pltpu.VMEM((rows, width), f32),
            pltpu.VMEM((sections, 2, width, width), bf16),
            pltpu.VMEM((sections, 2, width, width), bf16),
            dma((chunks,)),
            dma((2, chunks)),
            dma((sections, chunks)),
            dma((sections, chunks)),
            dma,
            dma((sections,)),
            dma((sections,)),
            dma((sections,)),
            dma((2, peers)),
            dma((2, peers)),
        ],
        compiler_params=pltpu.CompilerParams(
            collective_id=0, has_side_effects=True, vmem_limit_bytes=57 * 2**20
        ),
        cost_estimate=pl.CostEstimate(
            flops=flops, bytes_accessed=8 * rows * cols, transcendentals=0
        ),
    )(slab, leaf_y.T, leaf_t.T, tree_y, tree_t)
    bands = next(count for count in (16, 8, 4, 2, 1) if rows % (8 * count) == 0)
    return pl.pallas_call(
        functools.partial(place, bands, rows // bands),
        out_shape=jax.ShapeDtypeStruct(slab.shape, f32),
        in_specs=[hbm],
        out_specs=hbm,
        scratch_shapes=[pltpu.VMEM((bands, rows // bands, cols), f32), dma((bands,)), dma((bands,))],
        compiler_params=pltpu.CompilerParams(vmem_limit_bytes=57 * 2**20),
    )(mixed)


def solution(mesh):
    in_specs = (
        P("row", "col"),
        P("row", "col"),
        P("row", "col"),
        P(None, "row", None),
        P(None, "row", None),
    )
    out_specs = P("row", "col")
    return jax.shard_map(shards, mesh=mesh, in_specs=in_specs, out_specs=out_specs, check_vma=False)
```

```python
import functools

import jax
import jax.numpy as jnp
from jax import lax
from jax.experimental import pallas as pl
from jax.experimental.pallas import tpu as pltpu
from jax.sharding import PartitionSpec as P

MESH = pl.DeviceIdType.MESH


def halves(x):
    high = x.astype(jnp.bfloat16)
    return high, (x - high.astype(jnp.float32)).astype(jnp.bfloat16)


def wide(x):
    high, low = halves(x)
    return jnp.concatenate([high, high, low], axis=1)


def tall(x):
    high, low = halves(x)
    return jnp.concatenate([high, low, high], axis=0)


def product(left, right, dims=((1,), (0,))):
    return lax.dot_general(left, right, (dims, ((), ())), preferred_element_type=jnp.float32)


def kernel(
    sizes,
    slab_hbm, leaf_y_hbm, leaf_t_hbm, tree_y_hbm, tree_t_hbm,
    out_hbm,
    slab, head, part_out, part_in, tree_y, tree_t,
    gather_y, gather_t, y_t, v, v_sum, node_y_t, node_v,
    slab_sem, out_sem, part_send, part_recv, y_sem,
    t_local, t_send, t_recv, gather_send, gather_recv,
):
    peers, sections, chunks, width, chunk_cols, shard = sizes
    row, col = lax.axis_index("row"), lax.axis_index("col")
    partner = [jnp.bitwise_xor(row, 1 << s) for s in range(sections)]
    active = [lax.rem(row, 1 << s) == 0 for s in range(sections)]
    lower = [lax.rem(row, 2 << s) == 0 for s in range(sections)]

    def columns(c):
        return pl.ds(pl.multiple_of(c * chunk_cols, chunk_cols), chunk_cols)

    def slab_copy(c):
        return pltpu.make_async_copy(slab_hbm.at[:, columns(c)], slab.at[c], slab_sem.at[c])

    def tail_copy(c):
        return pltpu.make_async_copy(
            slab.at[c, pl.ds(width, width)], out_hbm.at[pl.ds(width, width), columns(c)], out_sem.at[1, c]
        )

    def head_copy(c):
        return pltpu.make_async_copy(
            head.at[c], out_hbm.at[pl.ds(0, width), columns(c)], out_sem.at[0, c]
        )

    def part_copy(s, c):
        return pltpu.make_async_remote_copy(
            src_ref=part_out.at[s, c], dst_ref=part_in.at[s, c],
            send_sem=part_send.at[s, c], recv_sem=part_recv.at[s, c],
            device_id={"row": partner[s]}, device_id_type=MESH,
        )

    def factor_copy(s):
        return pltpu.make_async_remote_copy(
            src_ref=tree_t_hbm.at[s], dst_ref=tree_t.at[s],
            send_sem=t_send.at[s], recv_sem=t_recv.at[s],
            device_id={"row": partner[s]}, device_id_type=MESH,
        )

    def factor_local(s):
        return pltpu.make_async_copy(tree_t_hbm.at[s], tree_t.at[s], t_local.at[s])

    short = peers % 2 == 0 and width % 256 == 0

    def of(owner):
        return pl.ds(pl.multiple_of(owner * shard, shard), shard)

    def y_shard(d):
        return pltpu.make_async_remote_copy(
            src_ref=gather_y.at[of(col)], dst_ref=gather_y.at[of(col)],
            send_sem=gather_send.at[0, d], recv_sem=gather_recv.at[0, d],
            device_id={"col": lax.rem(col + d, peers)}, device_id_type=MESH,
        )

    def t_shard(d, kept):
        block = gather_t.at[of(col), pl.ds(0, kept)]
        return pltpu.make_async_remote_copy(
            src_ref=block, dst_ref=block,
            send_sem=gather_send.at[1, d], recv_sem=gather_recv.at[1, d],
            device_id={"col": lax.rem(col + d, peers)}, device_id_type=MESH,
        )

    def by_shard(owner, act):
        if short:
            early = 2 * owner < peers
            pl.when(early)(lambda: act(width // 2))
            pl.when(jnp.logical_not(early))(lambda: act(width))
        else:
            act(width)

    barrier = pltpu.get_barrier_semaphore()
    for d in range(1, peers):
        pl.semaphore_signal(
            barrier, inc=1, device_id={"col": lax.rem(col + d, peers)}, device_id_type=MESH
        )
    for s in range(sections):
        pl.semaphore_signal(barrier, inc=1, device_id={"row": partner[s]}, device_id_type=MESH)

    own = [
        pltpu.make_async_copy(leaf_y_hbm, gather_y.at[of(col)], y_sem.at[1]),
        pltpu.make_async_copy(leaf_t_hbm, gather_t.at[of(col)], y_sem.at[2]),
    ]
    y_copy = pltpu.make_async_copy(tree_y_hbm, tree_y, y_sem.at[0])
    if short:
        gather_t[pl.ds(0, width // 2), pl.ds(width // 2, width // 2)] = jnp.zeros(
            (width // 2, width // 2), jnp.float32
        )
    for copy in own:
        copy.start()
    y_copy.start()
    for s in range(sections):
        pl.when(lower[s])(lambda s=s: factor_local(s).start())
    for copy in own:
        copy.wait()

    pl.semaphore_wait(barrier, peers - 1 + sections)
    for d in range(1, peers):
        y_shard(d).start()
    for d in range(1, peers):
        by_shard(col, lambda kept, d=d: t_shard(d, kept).start())
    for s in range(sections):
        pl.when(lower[s])(lambda s=s: factor_copy(s).start())

    for c in range(chunks):
        slab_copy(c).start()

    y_copy.wait()
    for s in range(sections):
        pl.when(lower[s])(lambda s=s: factor_local(s).wait())
        pl.when(jnp.logical_and(active[s], jnp.logical_not(lower[s])))(
            lambda s=s: factor_copy(s).wait_recv()
        )

        @pl.when(active[s])
        def _(s=s):
            vectors = tree_y[s]
            node_y_t[s] = wide(vectors.T)
            high, low = halves(tree_t[s])
            factor = jnp.concatenate([high, low, high], axis=1)
            node_v[s] = wide(product(wide(vectors), factor, ((1,), (1,))))

    for d in range(peers):
        owner = lax.rem(col - d + peers, peers)
        if d:
            y_shard(d).wait_recv()
        vectors = gather_y[of(owner), :]
        y_t[of(owner), :] = wide(vectors)
        turned = wide(vectors.T)
        if d:
            by_shard(owner, lambda kept, d=d: t_shard(d, kept).wait_recv())
        term = product(turned, tall(gather_t[of(owner), :]))
        total = v_sum[...] + term if d else term
        if d < peers - 1:
            v_sum[...] = total
        else:
            v[...] = wide(total)

    def send_part(s, c, rows):
        part_out[s, c] = product(node_y_t[s], tall(rows))
        part_copy(s, c).start()

    def leaf(c):
        slab_copy(c).wait()
        block = slab[c]
        coeffs = product(y_t[...], tall(block))
        updated = block - product(v[...], tall(coeffs))
        rows = updated[:width]
        head[c] = rows
        slab[c, width:, :] = updated[width:]
        tail_copy(c).start()
        send_part(0, c, rows)

    def node(s, c):
        part_copy(s, c).wait_recv()
        coeffs = part_out[s, c] + part_in[s, c]
        rows = head[c] - product(node_v[s], tall(coeffs))
        head[c] = rows
        if s + 1 < sections:
            pl.when(active[s + 1])(lambda: send_part(s + 1, c, rows))
            pl.when(jnp.logical_not(active[s + 1]))(lambda: head_copy(c).start())
        else:
            head_copy(c).start()

    lag = [1] + [3 + s for s in range(1, sections)]

    def step(t, carry):
        pl.when(t < chunks)(lambda: leaf(t))
        for s in range(sections):
            c = t - lag[s]
            inside = jnp.logical_and(c >= 0, c < chunks)
            pl.when(jnp.logical_and(active[s], inside))(lambda s=s, c=c: node(s, c))
        return carry

    lax.fori_loop(0, chunks + lag[-1], step, 0)

    def finish(c, carry):
        tail_copy(c).wait()
        head_copy(c).wait()
        for s in range(sections):
            pl.when(active[s])(lambda s=s: part_copy(s, c).wait_send())
        return carry

    lax.fori_loop(0, chunks, finish, 0)
    for d in range(1, peers):
        y_shard(d).wait_send()
        by_shard(col, lambda kept, d=d: t_shard(d, kept).wait_send())
    for s in range(sections):
        pl.when(lower[s])(lambda s=s: factor_copy(s).wait_send())


def place(bands, band, mixed_hbm, out_hbm, held, in_sem, out_sem):
    def copy_in(b):
        return pltpu.make_async_copy(mixed_hbm.at[pl.ds(b * band, band)], held.at[b], in_sem.at[b])

    def copy_out(b):
        return pltpu.make_async_copy(held.at[b], out_hbm.at[pl.ds(b * band, band)], out_sem.at[b])

    for b in range(bands):
        copy_in(b).start()
    for b in range(bands):
        copy_in(b).wait()
        copy_out(b).start()
    for b in range(bands):
        copy_out(b).wait()


def shards(slab, leaf_y, leaf_t, tree_y, tree_t):
    peers = lax.axis_size("col")
    rows, cols = slab.shape
    sections, width, _ = tree_y.shape
    shard = leaf_y.shape[1]
    chunk_cols = next(size for size in (256, 128) if cols % size == 0)
    chunks = cols // chunk_cols
    f32, bf16 = jnp.float32, jnp.bfloat16
    sizes = (peers, sections, chunks, width, chunk_cols, shard)
    dma = pltpu.SemaphoreType.DMA
    flops = 4 * cols * width * (rows + sections * width) * 3
    hbm = pl.BlockSpec(memory_space=pltpu.HBM)
    mixed = pl.pallas_call(
        functools.partial(kernel, sizes),
        out_shape=jax.ShapeDtypeStruct(slab.shape, f32),
        in_specs=[hbm] * 5,
        out_specs=hbm,
        scratch_shapes=[
            pltpu.VMEM((chunks, rows, chunk_cols), f32),
            pltpu.VMEM((chunks, width, chunk_cols), f32),
            pltpu.VMEM((sections, chunks, width, chunk_cols), f32),
            pltpu.VMEM((sections, chunks, width, chunk_cols), f32),
            pltpu.VMEM(tree_y.shape, f32),
            pltpu.VMEM(tree_t.shape, f32),
            pltpu.VMEM((width, rows), f32),
            pltpu.VMEM((width, width), f32),
            pltpu.VMEM((width, 3 * rows), bf16),
            pltpu.VMEM((rows, 3 * width), bf16),
            pltpu.VMEM((rows, width), f32),
            pltpu.VMEM((sections, width, 3 * width), bf16),
            pltpu.VMEM((sections, width, 3 * width), bf16),
            dma((chunks,)),
            dma((2, chunks)),
            dma((sections, chunks)),
            dma((sections, chunks)),
            dma((3,)),
            dma((sections,)),
            dma((sections,)),
            dma((sections,)),
            dma((2, peers)),
            dma((2, peers)),
        ],
        compiler_params=pltpu.CompilerParams(
            collective_id=0, has_side_effects=True, vmem_limit_bytes=57 * 2**20
        ),
        cost_estimate=pl.CostEstimate(
            flops=flops, bytes_accessed=8 * rows * cols, transcendentals=0
        ),
    )(slab, leaf_y.T, leaf_t.T, tree_y, tree_t)
    bands = next(count for count in (16, 8, 4, 2, 1) if rows % (8 * count) == 0)
    return pl.pallas_call(
        functools.partial(place, bands, rows // bands),
        out_shape=jax.ShapeDtypeStruct(slab.shape, f32),
        in_specs=[hbm],
        out_specs=hbm,
        scratch_shapes=[pltpu.VMEM((bands, rows // bands, cols), f32), dma((bands,)), dma((bands,))],
        compiler_params=pltpu.CompilerParams(vmem_limit_bytes=57 * 2**20),
    )(mixed)


def solution(mesh):
    in_specs = (
        P("row", "col"),
        P("row", "col"),
        P("row", "col"),
        P(None, "row", None),
        P(None, "row", None),
    )
    out_specs = P("row", "col")
    return jax.shard_map(shards, mesh=mesh, in_specs=in_specs, out_specs=out_specs, check_vma=False)
```

```python
import functools

import jax
import jax.numpy as jnp
from jax import lax
from jax.experimental import pallas as pl
from jax.experimental.pallas import tpu as pltpu
from jax.sharding import PartitionSpec as P

MESH = pl.DeviceIdType.MESH


def halves(x):
    high = x.astype(jnp.bfloat16)
    return high, (x - high.astype(jnp.float32)).astype(jnp.bfloat16)


def wide(x):
    high, low = halves(x)
    return jnp.concatenate([high, high, low], axis=1)


def tall(x):
    high, low = halves(x)
    return jnp.concatenate([high, low, high], axis=0)


def product(left, right, dims=((1,), (0,))):
    return lax.dot_general(left, right, (dims, ((), ())), preferred_element_type=jnp.float32)


def kernel(
    sizes,
    slab_hbm, leaf_y_hbm, leaf_t_hbm, tree_y_hbm, tree_t_hbm,
    out_hbm,
    slab, head, part_out, part_in, tree_y, tree_t,
    gather_y, gather_t, y_t, v, v_sum, node_y_t, node_v,
    slab_sem, out_sem, part_send, part_recv, y_sem,
    t_local, t_send, t_recv, gather_send, gather_recv,
):
    peers, sections, chunks, width, chunk_cols, shard = sizes
    row, col = lax.axis_index("row"), lax.axis_index("col")
    partner = [jnp.bitwise_xor(row, 1 << s) for s in range(sections)]
    active = [lax.rem(row, 1 << s) == 0 for s in range(sections)]
    lower = [lax.rem(row, 2 << s) == 0 for s in range(sections)]

    def columns(c):
        return pl.ds(pl.multiple_of(c * chunk_cols, chunk_cols), chunk_cols)

    def slab_copy(c):
        return pltpu.make_async_copy(slab_hbm.at[:, columns(c)], slab.at[c], slab_sem.at[c])

    def tail_copy(c):
        return pltpu.make_async_copy(
            slab.at[c, pl.ds(width, width)], out_hbm.at[pl.ds(width, width), columns(c)], out_sem.at[1, c]
        )

    def head_copy(c):
        return pltpu.make_async_copy(
            head.at[c], out_hbm.at[pl.ds(0, width), columns(c)], out_sem.at[0, c]
        )

    def part_copy(s, c):
        return pltpu.make_async_remote_copy(
            src_ref=part_out.at[s, c], dst_ref=part_in.at[s, c],
            send_sem=part_send.at[s, c], recv_sem=part_recv.at[s, c],
            device_id={"row": partner[s]}, device_id_type=MESH,
        )

    def factor_copy(s):
        return pltpu.make_async_remote_copy(
            src_ref=tree_t_hbm.at[s], dst_ref=tree_t.at[s],
            send_sem=t_send.at[s], recv_sem=t_recv.at[s],
            device_id={"row": partner[s]}, device_id_type=MESH,
        )

    def factor_local(s):
        return pltpu.make_async_copy(tree_t_hbm.at[s], tree_t.at[s], t_local.at[s])

    short = peers % 2 == 0 and width % 256 == 0

    def of(owner):
        return pl.ds(pl.multiple_of(owner * shard, shard), shard)

    def y_shard(d):
        return pltpu.make_async_remote_copy(
            src_ref=gather_y.at[of(col)], dst_ref=gather_y.at[of(col)],
            send_sem=gather_send.at[0, d], recv_sem=gather_recv.at[0, d],
            device_id={"col": lax.rem(col + d, peers)}, device_id_type=MESH,
        )

    def t_shard(d, kept):
        block = gather_t.at[of(col), pl.ds(0, kept)]
        return pltpu.make_async_remote_copy(
            src_ref=block, dst_ref=block,
            send_sem=gather_send.at[1, d], recv_sem=gather_recv.at[1, d],
            device_id={"col": lax.rem(col + d, peers)}, device_id_type=MESH,
        )

    def by_shard(owner, act):
        if short:
            early = 2 * owner < peers
            pl.when(early)(lambda: act(width // 2))
            pl.when(jnp.logical_not(early))(lambda: act(width))
        else:
            act(width)

    barrier = pltpu.get_barrier_semaphore()
    for d in range(1, peers):
        pl.semaphore_signal(
            barrier, inc=1, device_id={"col": lax.rem(col + d, peers)}, device_id_type=MESH
        )
    for s in range(sections):
        pl.semaphore_signal(barrier, inc=1, device_id={"row": partner[s]}, device_id_type=MESH)

    own = [
        pltpu.make_async_copy(leaf_y_hbm, gather_y.at[of(col)], y_sem.at[1]),
        pltpu.make_async_copy(leaf_t_hbm, gather_t.at[of(col)], y_sem.at[2]),
    ]
    y_copy = pltpu.make_async_copy(tree_y_hbm, tree_y, y_sem.at[0])
    if short:
        gather_t[pl.ds(0, width // 2), pl.ds(width // 2, width // 2)] = jnp.zeros(
            (width // 2, width // 2), jnp.float32
        )
    for copy in own:
        copy.start()
    y_copy.start()
    for s in range(sections):
        pl.when(lower[s])(lambda s=s: factor_local(s).start())
    for copy in own:
        copy.wait()

    pl.semaphore_wait(barrier, peers - 1 + sections)
    for d in range(1, peers):
        y_shard(d).start()
    for d in range(1, peers):
        by_shard(col, lambda kept, d=d: t_shard(d, kept).start())
    for s in range(sections):
        pl.when(lower[s])(lambda s=s: factor_copy(s).start())

    for c in range(chunks):
        slab_copy(c).start()

    y_copy.wait()
    for s in range(sections):
        pl.when(lower[s])(lambda s=s: factor_local(s).wait())
        pl.when(jnp.logical_and(active[s], jnp.logical_not(lower[s])))(
            lambda s=s: factor_copy(s).wait_recv()
        )

        node_y_t[s] = wide(tree_y[s].T)

        @pl.when(active[s])
        def _(s=s):
            vectors = tree_y[s]
            high, low = halves(tree_t[s])
            factor = jnp.concatenate([high, low, high], axis=1)
            node_v[s] = wide(product(wide(vectors), factor, ((1,), (1,))))

    for d in range(peers):
        owner = lax.rem(col - d + peers, peers)
        if d:
            y_shard(d).wait_recv()
        vectors = gather_y[of(owner), :]
        y_t[of(owner), :] = wide(vectors)
        turned = wide(vectors.T)
        if d:
            by_shard(owner, lambda kept, d=d: t_shard(d, kept).wait_recv())
        term = product(turned, tall(gather_t[of(owner), :]))
        total = v_sum[...] + term if d else term
        if d < peers - 1:
            v_sum[...] = total
        else:
            v[...] = wide(total)

    def work(leaf_chunk, nodes):
        if leaf_chunk is not None:
            slab_copy(leaf_chunk).wait()
        for s, c in nodes:
            part_copy(s, c).wait_recv()
        held = [(part_out[s, c] + part_in[s, c], head[c]) for s, c in nodes]
        block = None if leaf_chunk is None else slab[leaf_chunk]

        done = []
        for (s, c), (coeffs, rows) in zip(nodes, held):
            rows = rows - product(node_v[s], tall(coeffs))
            part = product(node_y_t[s + 1], tall(rows)) if s + 1 < sections else None
            done.append((rows, part))
        if leaf_chunk is not None:
            coeffs = product(y_t[...], tall(block))
            updated = block - product(v[...], tall(coeffs))
            leaf_part = product(node_y_t[0], tall(updated[:width]))

        for (s, c), (rows, part) in zip(nodes, done):
            head[c] = rows
            if part is None:
                head_copy(c).start()
                continue
            part_out[s + 1, c] = part
            pl.when(active[s + 1])(lambda s=s, c=c: part_copy(s + 1, c).start())
            pl.when(jnp.logical_not(active[s + 1]))(lambda c=c: head_copy(c).start())
        if leaf_chunk is not None:
            head[leaf_chunk] = updated[:width]
            part_out[0, leaf_chunk] = leaf_part
            part_copy(0, leaf_chunk).start()
            slab[leaf_chunk, width:, :] = updated[width:]
            tail_copy(leaf_chunk).start()

    lag = [3 * s for s in range(sections)]
    both = jnp.logical_and
    work(0, [])

    def step(t, carry):
        pl.when(t < chunks)(lambda: work(t, [(0, t - 1)]))
        pl.when(t == chunks)(lambda: work(None, [(0, t - 1)]))
        nodes = [(s, t - lag[s]) for s in range(1, sections)]
        inside = [both(c >= 0, c < chunks) for _, c in nodes]
        if nodes:
            every = functools.reduce(both, inside, active[sections - 1])
            pl.when(every)(lambda: work(None, nodes))
            for (s, c), within in zip(nodes, inside):
                alone = both(both(active[s], within), jnp.logical_not(every))
                pl.when(alone)(lambda s=s, c=c: work(None, [(s, c)]))
        return carry

    lax.fori_loop(1, chunks + max(lag[-1], 1), step, 0)

    def finish(c, carry):
        tail_copy(c).wait()
        head_copy(c).wait()
        for s in range(sections):
            pl.when(active[s])(lambda s=s: part_copy(s, c).wait_send())
        return carry

    lax.fori_loop(0, chunks, finish, 0)
    for d in range(1, peers):
        y_shard(d).wait_send()
        by_shard(col, lambda kept, d=d: t_shard(d, kept).wait_send())
    for s in range(sections):
        pl.when(lower[s])(lambda s=s: factor_copy(s).wait_send())


def place(bands, band, mixed_hbm, out_hbm, held, in_sem, out_sem):
    def copy_in(b):
        return pltpu.make_async_copy(mixed_hbm.at[pl.ds(b * band, band)], held.at[b], in_sem.at[b])

    def copy_out(b):
        return pltpu.make_async_copy(held.at[b], out_hbm.at[pl.ds(b * band, band)], out_sem.at[b])

    for b in range(bands):
        copy_in(b).start()
    for b in range(bands):
        copy_in(b).wait()
        copy_out(b).start()
    for b in range(bands):
        copy_out(b).wait()


def shards(slab, leaf_y, leaf_t, tree_y, tree_t):
    peers = lax.axis_size("col")
    rows, cols = slab.shape
    sections, width, _ = tree_y.shape
    shard = leaf_y.shape[1]
    chunk_cols = next(size for size in (256, 128) if cols % size == 0)
    chunks = cols // chunk_cols
    f32, bf16 = jnp.float32, jnp.bfloat16
    sizes = (peers, sections, chunks, width, chunk_cols, shard)
    dma = pltpu.SemaphoreType.DMA
    flops = 4 * cols * width * (rows + sections * width) * 3
    hbm = pl.BlockSpec(memory_space=pltpu.HBM)
    mixed = pl.pallas_call(
        functools.partial(kernel, sizes),
        out_shape=jax.ShapeDtypeStruct(slab.shape, f32),
        in_specs=[hbm] * 5,
        out_specs=hbm,
        scratch_shapes=[
            pltpu.VMEM((chunks, rows, chunk_cols), f32),
            pltpu.VMEM((chunks, width, chunk_cols), f32),
            pltpu.VMEM((sections, chunks, width, chunk_cols), f32),
            pltpu.VMEM((sections, chunks, width, chunk_cols), f32),
            pltpu.VMEM(tree_y.shape, f32),
            pltpu.VMEM(tree_t.shape, f32),
            pltpu.VMEM((width, rows), f32),
            pltpu.VMEM((width, width), f32),
            pltpu.VMEM((width, 3 * rows), bf16),
            pltpu.VMEM((rows, 3 * width), bf16),
            pltpu.VMEM((rows, width), f32),
            pltpu.VMEM((sections, width, 3 * width), bf16),
            pltpu.VMEM((sections, width, 3 * width), bf16),
            dma((chunks,)),
            dma((2, chunks)),
            dma((sections, chunks)),
            dma((sections, chunks)),
            dma((3,)),
            dma((sections,)),
            dma((sections,)),
            dma((sections,)),
            dma((2, peers)),
            dma((2, peers)),
        ],
        compiler_params=pltpu.CompilerParams(
            collective_id=0, has_side_effects=True, vmem_limit_bytes=57 * 2**20
        ),
        cost_estimate=pl.CostEstimate(
            flops=flops, bytes_accessed=8 * rows * cols, transcendentals=0
        ),
    )(slab, leaf_y.T, leaf_t.T, tree_y, tree_t)
    bands = next(count for count in (16, 8, 4, 2, 1) if rows % (8 * count) == 0)
    return pl.pallas_call(
        functools.partial(place, bands, rows // bands),
        out_shape=jax.ShapeDtypeStruct(slab.shape, f32),
        in_specs=[hbm],
        out_specs=hbm,
        scratch_shapes=[pltpu.VMEM((bands, rows // bands, cols), f32), dma((bands,)), dma((bands,))],
        compiler_params=pltpu.CompilerParams(vmem_limit_bytes=57 * 2**20),
    )(mixed)


def solution(mesh):
    in_specs = (
        P("row", "col"),
        P("row", "col"),
        P("row", "col"),
        P(None, "row", None),
        P(None, "row", None),
    )
    out_specs = P("row", "col")
    return jax.shard_map(shards, mesh=mesh, in_specs=in_specs, out_specs=out_specs, check_vma=False)
```

```python
import functools

import jax
import jax.numpy as jnp
from jax import lax
from jax.experimental import pallas as pl
from jax.experimental.pallas import tpu as pltpu
from jax.sharding import PartitionSpec as P

MESH = pl.DeviceIdType.MESH


def halves(x):
    high = x.astype(jnp.bfloat16)
    return high, (x - high.astype(jnp.float32)).astype(jnp.bfloat16)


def wide(x):
    high, low = halves(x)
    return jnp.concatenate([high, high, low], axis=1)


def tall(x):
    high, low = halves(x)
    return jnp.concatenate([high, low, high], axis=0)


def product(left, right, dims=((1,), (0,))):
    return lax.dot_general(left, right, (dims, ((), ())), preferred_element_type=jnp.float32)


def kernel(
    sizes,
    slab_hbm, leaf_y_hbm, leaf_t_hbm, tree_y_hbm, tree_t_hbm,
    out_hbm,
    slab, head, part_out, part_in, tree_y, tree_t,
    gather_y, gather_t, y_t, v, v_sum, node_y_t, node_v,
    slab_sem, out_sem, part_send, part_recv, y_sem,
    t_local, t_send, t_recv, gather_send, gather_recv,
):
    peers, sections, chunks, width, chunk_cols, shard = sizes
    row, col = lax.axis_index("row"), lax.axis_index("col")
    partner = [jnp.bitwise_xor(row, 1 << s) for s in range(sections)]
    active = [lax.rem(row, 1 << s) == 0 for s in range(sections)]
    lower = [lax.rem(row, 2 << s) == 0 for s in range(sections)]

    def columns(c):
        return pl.ds(pl.multiple_of(c * chunk_cols, chunk_cols), chunk_cols)

    def slab_copy(c):
        return pltpu.make_async_copy(slab_hbm.at[:, columns(c)], slab.at[c], slab_sem.at[c])

    def tail_copy(c):
        return pltpu.make_async_copy(
            slab.at[c, pl.ds(width, width)], out_hbm.at[pl.ds(width, width), columns(c)], out_sem.at[1, c]
        )

    def head_copy(c):
        return pltpu.make_async_copy(
            head.at[c], out_hbm.at[pl.ds(0, width), columns(c)], out_sem.at[0, c]
        )

    def part_copy(s, c):
        return pltpu.make_async_remote_copy(
            src_ref=part_out.at[s, c], dst_ref=part_in.at[s, c],
            send_sem=part_send.at[s, c], recv_sem=part_recv.at[s, c],
            device_id={"row": partner[s]}, device_id_type=MESH,
        )

    def factor_copy(s):
        return pltpu.make_async_remote_copy(
            src_ref=tree_t_hbm.at[s], dst_ref=tree_t.at[s],
            send_sem=t_send.at[s], recv_sem=t_recv.at[s],
            device_id={"row": partner[s]}, device_id_type=MESH,
        )

    def factor_local(s):
        return pltpu.make_async_copy(tree_t_hbm.at[s], tree_t.at[s], t_local.at[s])

    short = peers % 2 == 0 and width % 256 == 0

    def of(owner):
        return pl.ds(pl.multiple_of(owner * shard, shard), shard)

    def shard_copy(which, owner, way, to, kept=None):
        block = gather_t.at[of(owner), pl.ds(0, kept)] if which else gather_y.at[of(owner)]
        return pltpu.make_async_remote_copy(
            src_ref=block, dst_ref=block,
            send_sem=gather_send.at[which, way, owner], recv_sem=gather_recv.at[which, owner],
            device_id={"col": to}, device_id_type=MESH,
        )

    ahead = [col + 1, col - 1]
    behind = [col - 1, col + 1]
    open_way = [col < peers - 1, col > 0]

    def by_shard(owner, act):
        if short:
            early = 2 * owner < peers
            pl.when(early)(lambda: act(width // 2))
            pl.when(jnp.logical_not(early))(lambda: act(width))
        else:
            act(width)

    def shard_send(which, owner, way):
        def start(kept=None):
            shard_copy(which, owner, way, ahead[way], kept).start()

        pl.when(open_way[way])(lambda: by_shard(owner, start) if which else start())

    def shard_sent(which, owner, way):
        def wait(kept=None):
            shard_copy(which, owner, way, ahead[way], kept).wait_send()

        pl.when(open_way[way])(lambda: by_shard(owner, wait) if which else wait())

    def shard_arrived(which, owner, way):
        def wait(kept=None):
            shard_copy(which, owner, way, behind[way], kept).wait_recv()

        by_shard(owner, wait) if which else wait()

    barrier = pltpu.get_barrier_semaphore()
    for d in range(1, peers):
        pl.semaphore_signal(
            barrier, inc=1, device_id={"col": lax.rem(col + d, peers)}, device_id_type=MESH
        )
    for s in range(sections):
        pl.semaphore_signal(barrier, inc=1, device_id={"row": partner[s]}, device_id_type=MESH)

    own = [
        pltpu.make_async_copy(leaf_y_hbm, gather_y.at[of(col)], y_sem.at[1]),
        pltpu.make_async_copy(leaf_t_hbm, gather_t.at[of(col)], y_sem.at[2]),
    ]
    y_copy = pltpu.make_async_copy(tree_y_hbm, tree_y, y_sem.at[0])
    if short:
        gather_t[pl.ds(0, width // 2), pl.ds(width // 2, width // 2)] = jnp.zeros(
            (width // 2, width // 2), jnp.float32
        )
    for copy in own:
        copy.start()
    y_copy.start()
    for s in range(sections):
        pl.when(lower[s])(lambda s=s: factor_local(s).start())
    for copy in own:
        copy.wait()

    pl.semaphore_wait(barrier, peers - 1 + sections)
    for which in range(2):
        for way in range(2):
            shard_send(which, col, way)
    for s in range(sections):
        pl.when(lower[s])(lambda s=s: factor_copy(s).start())

    for c in range(chunks):
        slab_copy(c).start()

    y_copy.wait()
    for s in range(sections):
        pl.when(lower[s])(lambda s=s: factor_local(s).wait())
        pl.when(jnp.logical_and(active[s], jnp.logical_not(lower[s])))(
            lambda s=s: factor_copy(s).wait_recv()
        )

        node_y_t[s] = wide(tree_y[s].T)

        @pl.when(active[s])
        def _(s=s):
            vectors = tree_y[s]
            high, low = halves(tree_t[s])
            factor = jnp.concatenate([high, low, high], axis=1)
            node_v[s] = wide(product(wide(vectors), factor, ((1,), (1,))))

    def absorb(owner):
        vectors = gather_y[of(owner), :]
        y_t[of(owner), :] = wide(vectors)
        return product(wide(vectors.T), tall(gather_t[of(owner), :]))

    v_sum[...] = absorb(col)
    for far in range(1, peers):
        owners = [col - far, col + far]
        there = [owners[0] >= 0, owners[1] < peers]
        for which in range(2):
            for way in range(2):

                @pl.when(there[way])
                def _(which=which, way=way, owner=owners[way]):
                    shard_arrived(which, owner, way)
                    shard_send(which, owner, way)

        for way in range(2):

            @pl.when(there[way])
            def _(owner=owners[way]):
                v_sum[...] += absorb(owner)

    v[...] = wide(v_sum[...])

    def work(leaf_chunk, nodes):
        if leaf_chunk is not None:
            slab_copy(leaf_chunk).wait()
        for s, c in nodes:
            part_copy(s, c).wait_recv()
        held = [(part_out[s, c] + part_in[s, c], head[c]) for s, c in nodes]
        block = None if leaf_chunk is None else slab[leaf_chunk]

        done = []
        for (s, c), (coeffs, rows) in zip(nodes, held):
            rows = rows - product(node_v[s], tall(coeffs))
            part = product(node_y_t[s + 1], tall(rows)) if s + 1 < sections else None
            done.append((rows, part))
        if leaf_chunk is not None:
            coeffs = product(y_t[...], tall(block))
            updated = block - product(v[...], tall(coeffs))
            leaf_part = product(node_y_t[0], tall(updated[:width]))

        for (s, c), (rows, part) in zip(nodes, done):
            head[c] = rows
            if part is None:
                head_copy(c).start()
                continue
            part_out[s + 1, c] = part
            pl.when(active[s + 1])(lambda s=s, c=c: part_copy(s + 1, c).start())
            pl.when(jnp.logical_not(active[s + 1]))(lambda c=c: head_copy(c).start())
        if leaf_chunk is not None:
            head[leaf_chunk] = updated[:width]
            part_out[0, leaf_chunk] = leaf_part
            part_copy(0, leaf_chunk).start()
            slab[leaf_chunk, width:, :] = updated[width:]
            tail_copy(leaf_chunk).start()

    lag = [3 * s for s in range(sections)]
    both = jnp.logical_and
    work(0, [])

    def step(t, carry):
        pl.when(t < chunks)(lambda: work(t, [(0, t - 1)]))
        pl.when(t == chunks)(lambda: work(None, [(0, t - 1)]))
        nodes = [(s, t - lag[s]) for s in range(1, sections)]
        inside = [both(c >= 0, c < chunks) for _, c in nodes]
        if nodes:
            every = functools.reduce(both, inside, active[sections - 1])
            pl.when(every)(lambda: work(None, nodes))
            for (s, c), within in zip(nodes, inside):
                alone = both(both(active[s], within), jnp.logical_not(every))
                pl.when(alone)(lambda s=s, c=c: work(None, [(s, c)]))
        return carry

    lax.fori_loop(1, chunks + max(lag[-1], 1), step, 0)

    def finish(c, carry):
        tail_copy(c).wait()
        head_copy(c).wait()
        for s in range(sections):
            pl.when(active[s])(lambda s=s: part_copy(s, c).wait_send())
        return carry

    lax.fori_loop(0, chunks, finish, 0)
    for which in range(2):
        for way in range(2):
            shard_sent(which, col, way)
            for far in range(1, peers):
                owner = (col - far, col + far)[way]
                there = (owner >= 0, owner < peers)[way]
                pl.when(there)(lambda a=(which, owner, way): shard_sent(*a))
    for s in range(sections):
        pl.when(lower[s])(lambda s=s: factor_copy(s).wait_send())


def place(bands, band, mixed_hbm, out_hbm, sem):
    copies = [
        pltpu.make_async_copy(
            mixed_hbm.at[pl.ds(b * band, band)], out_hbm.at[pl.ds(b * band, band)], sem.at[b]
        )
        for b in range(bands)
    ]
    for copy in copies:
        copy.start()
    for copy in copies:
        copy.wait()


def shards(slab, leaf_y, leaf_t, tree_y, tree_t):
    peers = lax.axis_size("col")
    rows, cols = slab.shape
    sections, width, _ = tree_y.shape
    shard = leaf_y.shape[1]
    chunk_cols = next(size for size in (256, 128) if cols % size == 0)
    chunks = cols // chunk_cols
    f32, bf16 = jnp.float32, jnp.bfloat16
    sizes = (peers, sections, chunks, width, chunk_cols, shard)
    dma = pltpu.SemaphoreType.DMA
    flops = 4 * cols * width * (rows + sections * width) * 3
    hbm = pl.BlockSpec(memory_space=pltpu.HBM)
    mixed = pl.pallas_call(
        functools.partial(kernel, sizes),
        out_shape=jax.ShapeDtypeStruct(slab.shape, f32),
        in_specs=[hbm] * 5,
        out_specs=hbm,
        scratch_shapes=[
            pltpu.VMEM((chunks, rows, chunk_cols), f32),
            pltpu.VMEM((chunks, width, chunk_cols), f32),
            pltpu.VMEM((sections, chunks, width, chunk_cols), f32),
            pltpu.VMEM((sections, chunks, width, chunk_cols), f32),
            pltpu.VMEM(tree_y.shape, f32),
            pltpu.VMEM(tree_t.shape, f32),
            pltpu.VMEM((width, rows), f32),
            pltpu.VMEM((width, width), f32),
            pltpu.VMEM((width, 3 * rows), bf16),
            pltpu.VMEM((rows, 3 * width), bf16),
            pltpu.VMEM((rows, width), f32),
            pltpu.VMEM((sections, width, 3 * width), bf16),
            pltpu.VMEM((sections, width, 3 * width), bf16),
            dma((chunks,)),
            dma((2, chunks)),
            dma((sections, chunks)),
            dma((sections, chunks)),
            dma((3,)),
            dma((sections,)),
            dma((sections,)),
            dma((sections,)),
            dma((2, 2, peers)),
            dma((2, peers)),
        ],
        compiler_params=pltpu.CompilerParams(
            collective_id=0, has_side_effects=True, vmem_limit_bytes=57 * 2**20
        ),
        cost_estimate=pl.CostEstimate(
            flops=flops, bytes_accessed=8 * rows * cols, transcendentals=0
        ),
    )(slab, leaf_y.T, leaf_t.T, tree_y, tree_t)
    bands = next(count for count in (16, 8, 4, 2, 1) if rows % (8 * count) == 0)
    return pl.pallas_call(
        functools.partial(place, bands, rows // bands),
        out_shape=jax.ShapeDtypeStruct(slab.shape, f32),
        in_specs=[hbm],
        out_specs=hbm,
        scratch_shapes=[dma((bands,))],
        compiler_params=pltpu.CompilerParams(vmem_limit_bytes=57 * 2**20),
    )(mixed)


def solution(mesh):
    in_specs = (
        P("row", "col"),
        P("row", "col"),
        P("row", "col"),
        P(None, "row", None),
        P(None, "row", None),
    )
    out_specs = P("row", "col")
    return jax.shard_map(shards, mesh=mesh, in_specs=in_specs, out_specs=out_specs, check_vma=False)
```

```python
import functools

import jax
import jax.numpy as jnp
from jax import lax
from jax.experimental import pallas as pl
from jax.experimental.pallas import tpu as pltpu
from jax.sharding import PartitionSpec as P

MESH = pl.DeviceIdType.MESH


def halves(x):
    high = x.astype(jnp.bfloat16)
    return high, (x - high.astype(jnp.float32)).astype(jnp.bfloat16)


def wide(x):
    high, low = halves(x)
    return jnp.concatenate([high, high, low], axis=1)


def tall(x):
    high, low = halves(x)
    return jnp.concatenate([high, low, high], axis=0)


def product(left, right, dims=((1,), (0,))):
    return lax.dot_general(left, right, (dims, ((), ())), preferred_element_type=jnp.float32)


def kernel(
    sizes,
    slab_hbm, leaf_y_hbm, leaf_t_hbm, tree_y_hbm, tree_t_hbm,
    out_hbm,
    slab, slab_tall, head, part_out, part_in, tree_y, tree_t,
    gather_y, gather_t, y_t, v, v_sum, node_y_t, node_v,
    slab_sem, out_sem, part_send, part_recv, y_sem,
    t_local, t_send, t_recv, gather_send, gather_recv,
):
    peers, sections, chunks, width, chunk_cols, shard = sizes
    row, col = lax.axis_index("row"), lax.axis_index("col")
    partner = [jnp.bitwise_xor(row, 1 << s) for s in range(sections)]
    active = [lax.rem(row, 1 << s) == 0 for s in range(sections)]
    lower = [lax.rem(row, 2 << s) == 0 for s in range(sections)]

    def columns(c):
        return pl.ds(pl.multiple_of(c * chunk_cols, chunk_cols), chunk_cols)

    def slab_copy(c):
        return pltpu.make_async_copy(slab_hbm.at[:, columns(c)], slab.at[c], slab_sem.at[c])

    def tail_copy(c):
        return pltpu.make_async_copy(
            slab.at[c, pl.ds(width, width)], out_hbm.at[pl.ds(width, width), columns(c)], out_sem.at[1, c]
        )

    def head_copy(c):
        return pltpu.make_async_copy(
            head.at[c], out_hbm.at[pl.ds(0, width), columns(c)], out_sem.at[0, c]
        )

    def part_copy(s, c):
        return pltpu.make_async_remote_copy(
            src_ref=part_out.at[s, c], dst_ref=part_in.at[s, c],
            send_sem=part_send.at[s, c], recv_sem=part_recv.at[s, c],
            device_id={"row": partner[s]}, device_id_type=MESH,
        )

    def factor_copy(s):
        return pltpu.make_async_remote_copy(
            src_ref=tree_t_hbm.at[s], dst_ref=tree_t.at[s],
            send_sem=t_send.at[s], recv_sem=t_recv.at[s],
            device_id={"row": partner[s]}, device_id_type=MESH,
        )

    def factor_local(s):
        return pltpu.make_async_copy(tree_t_hbm.at[s], tree_t.at[s], t_local.at[s])

    short = peers % 2 == 0 and width % 256 == 0

    def of(owner):
        return pl.ds(pl.multiple_of(owner * shard, shard), shard)

    def shard_copy(which, owner, way, to, kept=None):
        block = gather_t.at[of(owner), pl.ds(0, kept)] if which else gather_y.at[of(owner)]
        return pltpu.make_async_remote_copy(
            src_ref=block, dst_ref=block,
            send_sem=gather_send.at[which, way, owner], recv_sem=gather_recv.at[which, owner],
            device_id={"col": to}, device_id_type=MESH,
        )

    ahead = [col + 1, col - 1]
    behind = [col - 1, col + 1]
    open_way = [col < peers - 1, col > 0]

    def by_shard(owner, act):
        if short:
            early = 2 * owner < peers
            pl.when(early)(lambda: act(width // 2))
            pl.when(jnp.logical_not(early))(lambda: act(width))
        else:
            act(width)

    def shard_send(which, owner, way):
        def start(kept=None):
            shard_copy(which, owner, way, ahead[way], kept).start()

        pl.when(open_way[way])(lambda: by_shard(owner, start) if which else start())

    def shard_sent(which, owner, way):
        def wait(kept=None):
            shard_copy(which, owner, way, ahead[way], kept).wait_send()

        pl.when(open_way[way])(lambda: by_shard(owner, wait) if which else wait())

    def shard_arrived(which, owner, way):
        def wait(kept=None):
            shard_copy(which, owner, way, behind[way], kept).wait_recv()

        by_shard(owner, wait) if which else wait()

    barrier = pltpu.get_barrier_semaphore()
    for d in range(1, peers):
        pl.semaphore_signal(
            barrier, inc=1, device_id={"col": lax.rem(col + d, peers)}, device_id_type=MESH
        )
    for s in range(sections):
        pl.semaphore_signal(barrier, inc=1, device_id={"row": partner[s]}, device_id_type=MESH)

    own = [
        pltpu.make_async_copy(leaf_y_hbm, gather_y.at[of(col)], y_sem.at[1]),
        pltpu.make_async_copy(leaf_t_hbm, gather_t.at[of(col)], y_sem.at[2]),
    ]
    y_copy = pltpu.make_async_copy(tree_y_hbm, tree_y, y_sem.at[0])
    if short:
        gather_t[pl.ds(0, width // 2), pl.ds(width // 2, width // 2)] = jnp.zeros(
            (width // 2, width // 2), jnp.float32
        )
    for copy in own:
        copy.start()
    y_copy.start()
    for s in range(sections):
        pl.when(lower[s])(lambda s=s: factor_local(s).start())
    for copy in own:
        copy.wait()

    pl.semaphore_wait(barrier, peers - 1 + sections)
    for which in range(2):
        for way in range(2):
            shard_send(which, col, way)
    for s in range(sections):
        pl.when(lower[s])(lambda s=s: factor_copy(s).start())

    for c in range(chunks):
        slab_copy(c).start()

    y_copy.wait()
    for s in range(sections):
        pl.when(lower[s])(lambda s=s: factor_local(s).wait())
        pl.when(jnp.logical_and(active[s], jnp.logical_not(lower[s])))(
            lambda s=s: factor_copy(s).wait_recv()
        )

        node_y_t[s] = wide(tree_y[s].T)

        @pl.when(active[s])
        def _(s=s):
            vectors = tree_y[s]
            high, low = halves(tree_t[s])
            factor = jnp.concatenate([high, low, high], axis=1)
            node_v[s] = wide(product(wide(vectors), factor, ((1,), (1,))))

    def absorb(owner):
        vectors = gather_y[of(owner), :]
        y_t[of(owner), :] = wide(vectors)
        return product(wide(vectors.T), tall(gather_t[of(owner), :]))

    def split(first, last):
        def one(c, carry):
            slab_copy(c).wait()
            slab_tall[c] = tall(slab[c])
            return carry

        lax.fori_loop(first, last, one, 0)

    rounds = max(peers - 2, 1)
    split_upto = [min(chunks, -(-chunks * far // rounds)) for far in range(peers)]
    v_sum[...] = absorb(col)
    for far in range(1, peers):
        owners = [col - far, col + far]
        there = [owners[0] >= 0, owners[1] < peers]
        for which in range(2):
            for way in range(2):

                @pl.when(there[way])
                def _(which=which, way=way, owner=owners[way]):
                    shard_arrived(which, owner, way)
                    shard_send(which, owner, way)

        split(split_upto[far - 1], split_upto[far])
        for way in range(2):

            @pl.when(there[way])
            def _(owner=owners[way]):
                v_sum[...] += absorb(owner)

    v[...] = wide(v_sum[...])

    def work(leaf_chunk, nodes):
        for s, c in nodes:
            part_copy(s, c).wait_recv()
        held = [(part_out[s, c] + part_in[s, c], head[c]) for s, c in nodes]
        block = None if leaf_chunk is None else slab[leaf_chunk]

        done = []
        for (s, c), (coeffs, rows) in zip(nodes, held):
            rows = rows - product(node_v[s], tall(coeffs))
            part = product(node_y_t[s + 1], tall(rows)) if s + 1 < sections else None
            done.append((rows, part))
        if leaf_chunk is not None:
            coeffs = product(y_t[...], slab_tall[leaf_chunk])
            updated = block - product(v[...], tall(coeffs))
            leaf_part = product(node_y_t[0], tall(updated[:width]))

        for (s, c), (rows, part) in zip(nodes, done):
            head[c] = rows
            if part is None:
                head_copy(c).start()
                continue
            part_out[s + 1, c] = part
            pl.when(active[s + 1])(lambda s=s, c=c: part_copy(s + 1, c).start())
            pl.when(jnp.logical_not(active[s + 1]))(lambda c=c: head_copy(c).start())
        if leaf_chunk is not None:
            head[leaf_chunk] = updated[:width]
            part_out[0, leaf_chunk] = leaf_part
            part_copy(0, leaf_chunk).start()
            slab[leaf_chunk, width:, :] = updated[width:]
            tail_copy(leaf_chunk).start()

    lag = [3 * s for s in range(sections)]
    both = jnp.logical_and
    work(0, [])

    def step(t, carry):
        pl.when(t < chunks)(lambda: work(t, [(0, t - 1)]))
        pl.when(t == chunks)(lambda: work(None, [(0, t - 1)]))
        nodes = [(s, t - lag[s]) for s in range(1, sections)]
        inside = [both(c >= 0, c < chunks) for _, c in nodes]
        if nodes:
            every = functools.reduce(both, inside, active[sections - 1])
            pl.when(every)(lambda: work(None, nodes))
            for (s, c), within in zip(nodes, inside):
                alone = both(both(active[s], within), jnp.logical_not(every))
                pl.when(alone)(lambda s=s, c=c: work(None, [(s, c)]))
        return carry

    lax.fori_loop(1, chunks + max(lag[-1], 1), step, 0)

    def finish(c, carry):
        tail_copy(c).wait()
        head_copy(c).wait()
        for s in range(sections):
            pl.when(active[s])(lambda s=s: part_copy(s, c).wait_send())
        return carry

    lax.fori_loop(0, chunks, finish, 0)
    for which in range(2):
        for way in range(2):
            shard_sent(which, col, way)
            for far in range(1, peers):
                owner = (col - far, col + far)[way]
                there = (owner >= 0, owner < peers)[way]
                pl.when(there)(lambda a=(which, owner, way): shard_sent(*a))
    for s in range(sections):
        pl.when(lower[s])(lambda s=s: factor_copy(s).wait_send())


def place(bands, band, mixed_hbm, out_hbm, held, in_sem, out_sem):
    def copy_in(b):
        return pltpu.make_async_copy(mixed_hbm.at[pl.ds(b * band, band)], held.at[b], in_sem.at[b])

    def copy_out(b):
        return pltpu.make_async_copy(held.at[b], out_hbm.at[pl.ds(b * band, band)], out_sem.at[b])

    window = min(8, bands)
    for b in range(window):
        copy_in(b).start()
    for b in range(bands):
        copy_in(b).wait()
        copy_out(b).start()
        if b + window < bands:
            copy_in(b + window).start()
    for b in range(bands):
        copy_out(b).wait()


def shards(slab, leaf_y, leaf_t, tree_y, tree_t):
    peers = lax.axis_size("col")
    rows, cols = slab.shape
    sections, width, _ = tree_y.shape
    shard = leaf_y.shape[1]
    chunk_cols = next(size for size in (256, 128) if cols % size == 0)
    chunks = cols // chunk_cols
    f32, bf16 = jnp.float32, jnp.bfloat16
    sizes = (peers, sections, chunks, width, chunk_cols, shard)
    dma = pltpu.SemaphoreType.DMA
    flops = 4 * cols * width * (rows + sections * width) * 3
    hbm = pl.BlockSpec(memory_space=pltpu.HBM)
    mixed = pl.pallas_call(
        functools.partial(kernel, sizes),
        out_shape=jax.ShapeDtypeStruct(slab.shape, f32),
        in_specs=[hbm] * 5,
        out_specs=hbm,
        scratch_shapes=[
            pltpu.VMEM((chunks, rows, chunk_cols), f32),
            pltpu.VMEM((chunks, 3 * rows, chunk_cols), bf16),
            pltpu.VMEM((chunks, width, chunk_cols), f32),
            pltpu.VMEM((sections, chunks, width, chunk_cols), f32),
            pltpu.VMEM((sections, chunks, width, chunk_cols), f32),
            pltpu.VMEM(tree_y.shape, f32),
            pltpu.VMEM(tree_t.shape, f32),
            pltpu.VMEM((width, rows), f32),
            pltpu.VMEM((width, width), f32),
            pltpu.VMEM((width, 3 * rows), bf16),
            pltpu.VMEM((rows, 3 * width), bf16),
            pltpu.VMEM((rows, width), f32),
            pltpu.VMEM((sections, width, 3 * width), bf16),
            pltpu.VMEM((sections, width, 3 * width), bf16),
            dma((chunks,)),
            dma((2, chunks)),
            dma((sections, chunks)),
            dma((sections, chunks)),
            dma((3,)),
            dma((sections,)),
            dma((sections,)),
            dma((sections,)),
            dma((2, 2, peers)),
            dma((2, peers)),
        ],
        compiler_params=pltpu.CompilerParams(
            collective_id=0, has_side_effects=True, vmem_limit_bytes=57 * 2**20
        ),
        cost_estimate=pl.CostEstimate(
            flops=flops, bytes_accessed=8 * rows * cols, transcendentals=0
        ),
    )(slab, leaf_y.T, leaf_t.T, tree_y, tree_t)
    bands = next(count for count in (16, 8, 4, 2, 1) if rows % (8 * count) == 0)
    return pl.pallas_call(
        functools.partial(place, bands, rows // bands),
        out_shape=jax.ShapeDtypeStruct(slab.shape, f32),
        in_specs=[hbm],
        out_specs=hbm,
        scratch_shapes=[pltpu.VMEM((bands, rows // bands, cols), f32), dma((bands,)), dma((bands,))],
        compiler_params=pltpu.CompilerParams(vmem_limit_bytes=57 * 2**20),
    )(mixed)


def solution(mesh):
    in_specs = (
        P("row", "col"),
        P("row", "col"),
        P("row", "col"),
        P(None, "row", None),
        P(None, "row", None),
    )
    out_specs = P("row", "col")
    return jax.shard_map(shards, mesh=mesh, in_specs=in_specs, out_specs=out_specs, check_vma=False)
```

```python
import functools

import jax
import jax.numpy as jnp
from jax import lax
from jax.experimental import pallas as pl
from jax.experimental.pallas import tpu as pltpu
from jax.sharding import PartitionSpec as P

MESH = pl.DeviceIdType.MESH


def halves(x):
    high = x.astype(jnp.bfloat16)
    return high, (x - high.astype(jnp.float32)).astype(jnp.bfloat16)


def wide(x):
    high, low = halves(x)
    return jnp.concatenate([high, high, low], axis=1)


def tall(x):
    high, low = halves(x)
    return jnp.concatenate([high, low, high], axis=0)


def product(left, right, dims=((1,), (0,))):
    return lax.dot_general(left, right, (dims, ((), ())), preferred_element_type=jnp.float32)


def kernel(
    sizes,
    slab_hbm, leaf_y_hbm, leaf_t_hbm, tree_y_hbm, tree_t_hbm,
    out_hbm,
    slab, slab_tall, head, part_out, part_in, tree_y, tree_t,
    gather_y, gather_t, y_t, v, v_sum, node_y_t, node_v,
    slab_sem, out_sem, part_send, part_recv, y_sem,
    t_local, t_send, t_recv, gather_send, gather_recv,
):
    peers, sections, chunks, width, chunk_cols, shard = sizes
    row, col = lax.axis_index("row"), lax.axis_index("col")
    partner = [jnp.bitwise_xor(row, 1 << s) for s in range(sections)]
    active = [lax.rem(row, 1 << s) == 0 for s in range(sections)]
    lower = [lax.rem(row, 2 << s) == 0 for s in range(sections)]

    def columns(c):
        return pl.ds(pl.multiple_of(c * chunk_cols, chunk_cols), chunk_cols)

    def slab_copy(c):
        return pltpu.make_async_copy(slab_hbm.at[:, columns(c)], slab.at[c], slab_sem.at[c])

    def tail_copy(c):
        return pltpu.make_async_copy(
            slab.at[c, pl.ds(width, width)], out_hbm.at[pl.ds(width, width), columns(c)], out_sem.at[1, c]
        )

    def head_copy(c):
        return pltpu.make_async_copy(
            head.at[c], out_hbm.at[pl.ds(0, width), columns(c)], out_sem.at[0, c]
        )

    def part_copy(s, c):
        return pltpu.make_async_remote_copy(
            src_ref=part_out.at[s, c], dst_ref=part_in.at[s, c],
            send_sem=part_send.at[s, c], recv_sem=part_recv.at[s, c],
            device_id={"row": partner[s]}, device_id_type=MESH,
        )

    def factor_copy(s):
        return pltpu.make_async_remote_copy(
            src_ref=tree_t_hbm.at[s], dst_ref=tree_t.at[s],
            send_sem=t_send.at[s], recv_sem=t_recv.at[s],
            device_id={"row": partner[s]}, device_id_type=MESH,
        )

    def factor_local(s):
        return pltpu.make_async_copy(tree_t_hbm.at[s], tree_t.at[s], t_local.at[s])

    short = peers % 2 == 0 and width % 256 == 0

    def of(owner):
        return pl.ds(pl.multiple_of(owner * shard, shard), shard)

    def shard_copy(which, owner, way, to, kept=None):
        block = gather_t.at[of(owner), pl.ds(0, kept)] if which else gather_y.at[of(owner)]
        return pltpu.make_async_remote_copy(
            src_ref=block, dst_ref=block,
            send_sem=gather_send.at[which, way, owner], recv_sem=gather_recv.at[which, owner],
            device_id={"col": to}, device_id_type=MESH,
        )

    ahead = [col + 1, col - 1]
    behind = [col - 1, col + 1]
    open_way = [col < peers - 1, col > 0]

    def by_shard(owner, act):
        if short:
            early = 2 * owner < peers
            pl.when(early)(lambda: act(width // 2))
            pl.when(jnp.logical_not(early))(lambda: act(width))
        else:
            act(width)

    def shard_send(which, owner, way):
        def start(kept=None):
            shard_copy(which, owner, way, ahead[way], kept).start()

        pl.when(open_way[way])(lambda: by_shard(owner, start) if which else start())

    def shard_sent(which, owner, way):
        def wait(kept=None):
            shard_copy(which, owner, way, ahead[way], kept).wait_send()

        pl.when(open_way[way])(lambda: by_shard(owner, wait) if which else wait())

    def shard_arrived(which, owner, way):
        def wait(kept=None):
            shard_copy(which, owner, way, behind[way], kept).wait_recv()

        by_shard(owner, wait) if which else wait()

    barrier = pltpu.get_barrier_semaphore()
    for d in range(1, peers):
        pl.semaphore_signal(
            barrier, inc=1, device_id={"col": lax.rem(col + d, peers)}, device_id_type=MESH
        )
    for s in range(sections):
        pl.semaphore_signal(barrier, inc=1, device_id={"row": partner[s]}, device_id_type=MESH)

    own = [
        pltpu.make_async_copy(leaf_y_hbm, gather_y.at[of(col)], y_sem.at[1]),
        pltpu.make_async_copy(leaf_t_hbm, gather_t.at[of(col)], y_sem.at[2]),
    ]
    y_copy = pltpu.make_async_copy(tree_y_hbm, tree_y, y_sem.at[0])
    if short:
        gather_t[pl.ds(0, width // 2), pl.ds(width // 2, width // 2)] = jnp.zeros(
            (width // 2, width // 2), jnp.float32
        )
    for copy in own:
        copy.start()
    y_copy.start()
    for s in range(sections):
        pl.when(lower[s])(lambda s=s: factor_local(s).start())
    for copy in own:
        copy.wait()

    pl.semaphore_wait(barrier, peers - 1 + sections)
    for which in range(2):
        for way in range(2):
            shard_send(which, col, way)
    for s in range(sections):
        pl.when(lower[s])(lambda s=s: factor_copy(s).start())

    for c in range(chunks):
        slab_copy(c).start()

    y_copy.wait()
    for s in range(sections):
        pl.when(lower[s])(lambda s=s: factor_local(s).wait())
        pl.when(jnp.logical_and(active[s], jnp.logical_not(lower[s])))(
            lambda s=s: factor_copy(s).wait_recv()
        )

        node_y_t[s] = wide(tree_y[s].T)

        @pl.when(active[s])
        def _(s=s):
            vectors = tree_y[s]
            high, low = halves(tree_t[s])
            factor = jnp.concatenate([high, low, high], axis=1)
            node_v[s] = wide(product(wide(vectors), factor, ((1,), (1,))))

    def absorb(owner):
        vectors = gather_y[of(owner), :]
        y_t[of(owner), :] = wide(vectors)
        return product(wide(vectors.T), tall(gather_t[of(owner), :]))

    def split(first, last):
        def one(c, carry):
            slab_copy(c).wait()
            slab_tall[c] = tall(slab[c])
            return carry

        lax.fori_loop(first, last, one, 0)

    rounds = max(peers - 2, 1)
    split_upto = [min(chunks, -(-chunks * far // rounds)) for far in range(peers)]
    v_sum[...] = absorb(col)
    for far in range(1, peers):
        owners = [col - far, col + far]
        there = [owners[0] >= 0, owners[1] < peers]
        for which in range(2):
            for way in range(2):

                @pl.when(there[way])
                def _(which=which, way=way, owner=owners[way]):
                    shard_arrived(which, owner, way)
                    shard_send(which, owner, way)

        split(split_upto[far - 1], split_upto[far])
        for way in range(2):

            @pl.when(there[way])
            def _(owner=owners[way]):
                v_sum[...] += absorb(owner)

    v[...] = wide(v_sum[...])

    def work(leaf_chunk, nodes):
        for s, c in nodes:
            part_copy(s, c).wait_recv()
        held = [(part_out[s, c] + part_in[s, c], head[c]) for s, c in nodes]
        block = None if leaf_chunk is None else slab[leaf_chunk]

        done = []
        for (s, c), (coeffs, rows) in zip(nodes, held):
            rows = rows - product(node_v[s], tall(coeffs))
            part = product(node_y_t[s + 1], tall(rows)) if s + 1 < sections else None
            done.append((rows, part))
        if leaf_chunk is not None:
            coeffs = product(y_t[...], slab_tall[leaf_chunk])
            updated = block - product(v[...], tall(coeffs))
            leaf_part = product(node_y_t[0], tall(updated[:width]))

        for (s, c), (rows, part) in zip(nodes, done):
            head[c] = rows
            if part is None:
                head_copy(c).start()
                continue
            part_out[s + 1, c] = part
            pl.when(active[s + 1])(lambda s=s, c=c: part_copy(s + 1, c).start())
            pl.when(jnp.logical_not(active[s + 1]))(lambda c=c: head_copy(c).start())
        if leaf_chunk is not None:
            head[leaf_chunk] = updated[:width]
            part_out[0, leaf_chunk] = leaf_part
            part_copy(0, leaf_chunk).start()
            slab[leaf_chunk, width:, :] = updated[width:]
            tail_copy(leaf_chunk).start()

    lag = [1] + [3 * s - 1 for s in range(1, sections)]
    both = jnp.logical_and
    for c in range(min(2, chunks)):
        work(c, [])

    def step(t, carry):
        pl.when(t <= chunks)(lambda: work(None, [(0, t - 1)]))
        pl.when(t + 1 < chunks)(lambda: work(t + 1, []))
        nodes = [(s, t - lag[s]) for s in range(1, sections)]
        inside = [both(c >= 0, c < chunks) for _, c in nodes]
        if nodes:
            every = functools.reduce(both, inside, active[sections - 1])
            pl.when(every)(lambda: work(None, nodes))
            for (s, c), within in zip(nodes, inside):
                alone = both(both(active[s], within), jnp.logical_not(every))
                pl.when(alone)(lambda s=s, c=c: work(None, [(s, c)]))
        return carry

    lax.fori_loop(1, chunks + lag[-1], step, 0)

    def finish(c, carry):
        tail_copy(c).wait()
        head_copy(c).wait()
        for s in range(sections):
            pl.when(active[s])(lambda s=s: part_copy(s, c).wait_send())
        return carry

    lax.fori_loop(0, chunks, finish, 0)
    for which in range(2):
        for way in range(2):
            shard_sent(which, col, way)
            for far in range(1, peers):
                owner = (col - far, col + far)[way]
                there = (owner >= 0, owner < peers)[way]
                pl.when(there)(lambda a=(which, owner, way): shard_sent(*a))
    for s in range(sections):
        pl.when(lower[s])(lambda s=s: factor_copy(s).wait_send())


def place(bands, band, mixed_hbm, out_hbm, held, in_sem, out_sem):
    def copy_in(b):
        return pltpu.make_async_copy(mixed_hbm.at[pl.ds(b * band, band)], held.at[b], in_sem.at[b])

    def copy_out(b):
        return pltpu.make_async_copy(held.at[b], out_hbm.at[pl.ds(b * band, band)], out_sem.at[b])

    window = min(8, bands)
    for b in range(window):
        copy_in(b).start()
    for b in range(bands):
        copy_in(b).wait()
        copy_out(b).start()
        if b + window < bands:
            copy_in(b + window).start()
    for b in range(bands):
        copy_out(b).wait()


def shards(slab, leaf_y, leaf_t, tree_y, tree_t):
    peers = lax.axis_size("col")
    rows, cols = slab.shape
    sections, width, _ = tree_y.shape
    shard = leaf_y.shape[1]
    chunk_cols = next(size for size in (256, 128) if cols % size == 0)
    chunks = cols // chunk_cols
    f32, bf16 = jnp.float32, jnp.bfloat16
    sizes = (peers, sections, chunks, width, chunk_cols, shard)
    dma = pltpu.SemaphoreType.DMA
    flops = 4 * cols * width * (rows + sections * width) * 3
    hbm = pl.BlockSpec(memory_space=pltpu.HBM)
    mixed = pl.pallas_call(
        functools.partial(kernel, sizes),
        out_shape=jax.ShapeDtypeStruct(slab.shape, f32),
        in_specs=[hbm] * 5,
        out_specs=hbm,
        scratch_shapes=[
            pltpu.VMEM((chunks, rows, chunk_cols), f32),
            pltpu.VMEM((chunks, 3 * rows, chunk_cols), bf16),
            pltpu.VMEM((chunks, width, chunk_cols), f32),
            pltpu.VMEM((sections, chunks, width, chunk_cols), f32),
            pltpu.VMEM((sections, chunks, width, chunk_cols), f32),
            pltpu.VMEM(tree_y.shape, f32),
            pltpu.VMEM(tree_t.shape, f32),
            pltpu.VMEM((width, rows), f32),
            pltpu.VMEM((width, width), f32),
            pltpu.VMEM((width, 3 * rows), bf16),
            pltpu.VMEM((rows, 3 * width), bf16),
            pltpu.VMEM((rows, width), f32),
            pltpu.VMEM((sections, width, 3 * width), bf16),
            pltpu.VMEM((sections, width, 3 * width), bf16),
            dma((chunks,)),
            dma((2, chunks)),
            dma((sections, chunks)),
            dma((sections, chunks)),
            dma((3,)),
            dma((sections,)),
            dma((sections,)),
            dma((sections,)),
            dma((2, 2, peers)),
            dma((2, peers)),
        ],
        compiler_params=pltpu.CompilerParams(
            collective_id=0, has_side_effects=True, vmem_limit_bytes=57 * 2**20
        ),
        cost_estimate=pl.CostEstimate(
            flops=flops, bytes_accessed=8 * rows * cols, transcendentals=0
        ),
    )(slab, leaf_y.T, leaf_t.T, tree_y, tree_t)
    bands = next(count for count in (16, 8, 4, 2, 1) if rows % (8 * count) == 0)
    return pl.pallas_call(
        functools.partial(place, bands, rows // bands),
        out_shape=jax.ShapeDtypeStruct(slab.shape, f32),
        in_specs=[hbm],
        out_specs=hbm,
        scratch_shapes=[pltpu.VMEM((bands, rows // bands, cols), f32), dma((bands,)), dma((bands,))],
        compiler_params=pltpu.CompilerParams(vmem_limit_bytes=57 * 2**20),
    )(mixed)


def solution(mesh):
    in_specs = (
        P("row", "col"),
        P("row", "col"),
        P("row", "col"),
        P(None, "row", None),
        P(None, "row", None),
    )
    out_specs = P("row", "col")
    return jax.shard_map(shards, mesh=mesh, in_specs=in_specs, out_specs=out_specs, check_vma=False)
```

```python
import functools

import jax
import jax.numpy as jnp
from jax import lax
from jax.experimental import pallas as pl
from jax.experimental.pallas import tpu as pltpu
from jax.sharding import PartitionSpec as P

MESH = pl.DeviceIdType.MESH


def halves(x):
    high = x.astype(jnp.bfloat16)
    return high, (x - high.astype(jnp.float32)).astype(jnp.bfloat16)


def stacked(x):
    return jnp.concatenate(halves(x), axis=0)


def product(left, right):
    def one(a, b):
        return jnp.dot(a, b, preferred_element_type=jnp.float32)

    rows, depth = left.shape[0] // 2, left.shape[1]
    main = one(left, right[:depth])
    return main[:rows] + (main[rows:] + one(left[:rows], right[depth:]))


def kernel(
    sizes,
    slab_hbm, leaf_y_hbm, leaf_t_hbm, tree_y_hbm, tree_t_hbm,
    out_hbm,
    slab, slab_tall, head, part_out, part_in, tree_y, tree_t,
    gather_y, gather_t, y_t, v, v_sum, node_y_t, node_v,
    slab_sem, out_sem, part_send, part_recv, y_sem,
    t_local, t_send, t_recv, gather_send, gather_recv,
):
    peers, sections, chunks, width, chunk_cols, shard = sizes
    row, col = lax.axis_index("row"), lax.axis_index("col")
    partner = [jnp.bitwise_xor(row, 1 << s) for s in range(sections)]
    active = [lax.rem(row, 1 << s) == 0 for s in range(sections)]
    lower = [lax.rem(row, 2 << s) == 0 for s in range(sections)]

    def columns(c):
        return pl.ds(pl.multiple_of(c * chunk_cols, chunk_cols), chunk_cols)

    def slab_copy(c):
        return pltpu.make_async_copy(slab_hbm.at[:, columns(c)], slab.at[c], slab_sem.at[c])

    def tail_copy(c):
        return pltpu.make_async_copy(
            slab.at[c, pl.ds(width, width)], out_hbm.at[pl.ds(width, width), columns(c)], out_sem.at[1, c]
        )

    def head_copy(c):
        return pltpu.make_async_copy(
            head.at[c], out_hbm.at[pl.ds(0, width), columns(c)], out_sem.at[0, c]
        )

    def part_copy(s, c):
        return pltpu.make_async_remote_copy(
            src_ref=part_out.at[s, c], dst_ref=part_in.at[s, c],
            send_sem=part_send.at[s, c], recv_sem=part_recv.at[s, c],
            device_id={"row": partner[s]}, device_id_type=MESH,
        )

    def factor_copy(s):
        return pltpu.make_async_remote_copy(
            src_ref=tree_t_hbm.at[s], dst_ref=tree_t.at[s],
            send_sem=t_send.at[s], recv_sem=t_recv.at[s],
            device_id={"row": partner[s]}, device_id_type=MESH,
        )

    def factor_local(s):
        return pltpu.make_async_copy(tree_t_hbm.at[s], tree_t.at[s], t_local.at[s])

    short = peers % 2 == 0 and width % 256 == 0

    def of(owner):
        return pl.ds(pl.multiple_of(owner * shard, shard), shard)

    def shard_copy(which, owner, way, to, kept=None):
        block = gather_t.at[of(owner), pl.ds(0, kept)] if which else gather_y.at[of(owner)]
        return pltpu.make_async_remote_copy(
            src_ref=block, dst_ref=block,
            send_sem=gather_send.at[which, way, owner], recv_sem=gather_recv.at[which, owner],
            device_id={"col": to}, device_id_type=MESH,
        )

    ahead = [col + 1, col - 1]
    behind = [col - 1, col + 1]
    open_way = [col < peers - 1, col > 0]

    def by_shard(owner, act):
        if short:
            early = 2 * owner < peers
            pl.when(early)(lambda: act(width // 2))
            pl.when(jnp.logical_not(early))(lambda: act(width))
        else:
            act(width)

    def shard_send(which, owner, way):
        def start(kept=None):
            shard_copy(which, owner, way, ahead[way], kept).start()

        pl.when(open_way[way])(lambda: by_shard(owner, start) if which else start())

    def shard_sent(which, owner, way):
        def wait(kept=None):
            shard_copy(which, owner, way, ahead[way], kept).wait_send()

        pl.when(open_way[way])(lambda: by_shard(owner, wait) if which else wait())

    def shard_arrived(which, owner, way):
        def wait(kept=None):
            shard_copy(which, owner, way, behind[way], kept).wait_recv()

        by_shard(owner, wait) if which else wait()

    barrier = pltpu.get_barrier_semaphore()
    for d in range(1, peers):
        pl.semaphore_signal(
            barrier, inc=1, device_id={"col": lax.rem(col + d, peers)}, device_id_type=MESH
        )
    for s in range(sections):
        pl.semaphore_signal(barrier, inc=1, device_id={"row": partner[s]}, device_id_type=MESH)

    own = [
        pltpu.make_async_copy(leaf_y_hbm, gather_y.at[of(col)], y_sem.at[1]),
        pltpu.make_async_copy(leaf_t_hbm, gather_t.at[of(col)], y_sem.at[2]),
    ]
    y_copy = pltpu.make_async_copy(tree_y_hbm, tree_y, y_sem.at[0])
    if short:
        gather_t[pl.ds(0, width // 2), pl.ds(width // 2, width // 2)] = jnp.zeros(
            (width // 2, width // 2), jnp.float32
        )
    for copy in own:
        copy.start()
    y_copy.start()
    for s in range(sections):
        pl.when(lower[s])(lambda s=s: factor_local(s).start())
    for copy in own:
        copy.wait()

    pl.semaphore_wait(barrier, peers - 1 + sections)
    for which in range(2):
        for way in range(2):
            shard_send(which, col, way)
    for s in range(sections):
        pl.when(lower[s])(lambda s=s: factor_copy(s).start())

    for c in range(chunks):
        slab_copy(c).start()

    y_copy.wait()
    for s in range(sections):
        pl.when(lower[s])(lambda s=s: factor_local(s).wait())
        pl.when(jnp.logical_and(active[s], jnp.logical_not(lower[s])))(
            lambda s=s: factor_copy(s).wait_recv()
        )

        node_y_t[s] = stacked(tree_y[s].T)

        @pl.when(active[s])
        def _(s=s):
            vectors = tree_y[s]
            node_v[s] = stacked(product(stacked(vectors), stacked(tree_t[s].T)))

    def absorb(owner):
        vectors = gather_y[of(owner), :]
        y_t[0, of(owner), :], y_t[1, of(owner), :] = halves(vectors)
        return product(stacked(vectors.T), stacked(gather_t[of(owner), :]))

    def split(first, last):
        def one(c, carry):
            slab_copy(c).wait()
            slab_tall[c] = stacked(slab[c])
            return carry

        lax.fori_loop(first, last, one, 0)

    rounds = max(peers - 2, 1)
    split_upto = [min(chunks, -(-chunks * far // rounds)) for far in range(peers)]
    v_sum[...] = absorb(col)
    for far in range(1, peers):
        owners = [col - far, col + far]
        there = [owners[0] >= 0, owners[1] < peers]
        for which in range(2):
            for way in range(2):

                @pl.when(there[way])
                def _(which=which, way=way, owner=owners[way]):
                    shard_arrived(which, owner, way)
                    shard_send(which, owner, way)

        split(split_upto[far - 1], split_upto[far])
        for way in range(2):

            @pl.when(there[way])
            def _(owner=owners[way]):
                v_sum[...] += absorb(owner)

    v[...] = stacked(v_sum[...])

    def work(leaf_chunk, nodes):
        for s, c in nodes:
            part_copy(s, c).wait_recv()
        held = [(part_out[s, c] + part_in[s, c], head[c]) for s, c in nodes]
        block = None if leaf_chunk is None else slab[leaf_chunk]

        done = []
        for (s, c), (coeffs, rows) in zip(nodes, held):
            rows = rows - product(node_v[s], stacked(coeffs))
            part = product(node_y_t[s + 1], stacked(rows)) if s + 1 < sections else None
            done.append((rows, part))
        if leaf_chunk is not None:
            coeffs = product(y_t[...].reshape(2 * width, -1), slab_tall[leaf_chunk])
            updated = block - product(v[...], stacked(coeffs))
            leaf_part = product(node_y_t[0], stacked(updated[:width]))

        for (s, c), (rows, part) in zip(nodes, done):
            head[c] = rows
            if part is None:
                head_copy(c).start()
                continue
            part_out[s + 1, c] = part
            pl.when(active[s + 1])(lambda s=s, c=c: part_copy(s + 1, c).start())
            pl.when(jnp.logical_not(active[s + 1]))(lambda c=c: head_copy(c).start())
        if leaf_chunk is not None:
            head[leaf_chunk] = updated[:width]
            part_out[0, leaf_chunk] = leaf_part
            part_copy(0, leaf_chunk).start()
            slab[leaf_chunk, width:, :] = updated[width:]
            tail_copy(leaf_chunk).start()

    lag = [3 * s for s in range(sections)]
    both = jnp.logical_and
    work(0, [])

    def step(t, carry):
        pl.when(t < chunks)(lambda: work(t, [(0, t - 1)]))
        pl.when(t == chunks)(lambda: work(None, [(0, t - 1)]))
        nodes = [(s, t - lag[s]) for s in range(1, sections)]
        inside = [both(c >= 0, c < chunks) for _, c in nodes]
        if nodes:
            every = functools.reduce(both, inside, active[sections - 1])
            pl.when(every)(lambda: work(None, nodes))
            for (s, c), within in zip(nodes, inside):
                alone = both(both(active[s], within), jnp.logical_not(every))
                pl.when(alone)(lambda s=s, c=c: work(None, [(s, c)]))
        return carry

    lax.fori_loop(1, chunks + max(lag[-1], 1), step, 0)

    def finish(c, carry):
        tail_copy(c).wait()
        head_copy(c).wait()
        for s in range(sections):
            pl.when(active[s])(lambda s=s: part_copy(s, c).wait_send())
        return carry

    lax.fori_loop(0, chunks, finish, 0)
    for which in range(2):
        for way in range(2):
            shard_sent(which, col, way)
            for far in range(1, peers):
                owner = (col - far, col + far)[way]
                there = (owner >= 0, owner < peers)[way]
                pl.when(there)(lambda a=(which, owner, way): shard_sent(*a))
    for s in range(sections):
        pl.when(lower[s])(lambda s=s: factor_copy(s).wait_send())


def place(bands, band, mixed_hbm, out_hbm, held, in_sem, out_sem):
    def copy_in(b):
        return pltpu.make_async_copy(mixed_hbm.at[pl.ds(b * band, band)], held.at[b], in_sem.at[b])

    def copy_out(b):
        return pltpu.make_async_copy(held.at[b], out_hbm.at[pl.ds(b * band, band)], out_sem.at[b])

    window = min(8, bands)
    for b in range(window):
        copy_in(b).start()
    for b in range(bands):
        copy_in(b).wait()
        copy_out(b).start()
        if b + window < bands:
            copy_in(b + window).start()
    for b in range(bands):
        copy_out(b).wait()


def shards(slab, leaf_y, leaf_t, tree_y, tree_t):
    peers = lax.axis_size("col")
    rows, cols = slab.shape
    sections, width, _ = tree_y.shape
    shard = leaf_y.shape[1]
    chunk_cols = next(size for size in (256, 128) if cols % size == 0)
    chunks = cols // chunk_cols
    f32, bf16 = jnp.float32, jnp.bfloat16
    sizes = (peers, sections, chunks, width, chunk_cols, shard)
    dma = pltpu.SemaphoreType.DMA
    flops = 4 * cols * width * (rows + sections * width) * 3
    hbm = pl.BlockSpec(memory_space=pltpu.HBM)
    mixed = pl.pallas_call(
        functools.partial(kernel, sizes),
        out_shape=jax.ShapeDtypeStruct(slab.shape, f32),
        in_specs=[hbm] * 5,
        out_specs=hbm,
        scratch_shapes=[
            pltpu.VMEM((chunks, rows, chunk_cols), f32),
            pltpu.VMEM((chunks, 2 * rows, chunk_cols), bf16),
            pltpu.VMEM((chunks, width, chunk_cols), f32),
            pltpu.VMEM((sections, chunks, width, chunk_cols), f32),
            pltpu.VMEM((sections, chunks, width, chunk_cols), f32),
            pltpu.VMEM(tree_y.shape, f32),
            pltpu.VMEM(tree_t.shape, f32),
            pltpu.VMEM((width, rows), f32),
            pltpu.VMEM((width, width), f32),
            pltpu.VMEM((2, width, rows), bf16),
            pltpu.VMEM((2 * rows, width), bf16),
            pltpu.VMEM((rows, width), f32),
            pltpu.VMEM((sections, 2 * width, width), bf16),
            pltpu.VMEM((sections, 2 * width, width), bf16),
            dma((chunks,)),
            dma((2, chunks)),
            dma((sections, chunks)),
            dma((sections, chunks)),
            dma((3,)),
            dma((sections,)),
            dma((sections,)),
            dma((sections,)),
            dma((2, 2, peers)),
            dma((2, peers)),
        ],
        compiler_params=pltpu.CompilerParams(
            collective_id=0, has_side_effects=True, vmem_limit_bytes=57 * 2**20
        ),
        cost_estimate=pl.CostEstimate(
            flops=flops, bytes_accessed=8 * rows * cols, transcendentals=0
        ),
    )(slab, leaf_y.T, leaf_t.T, tree_y, tree_t)
    bands = next(count for count in (16, 8, 4, 2, 1) if rows % (8 * count) == 0)
    return pl.pallas_call(
        functools.partial(place, bands, rows // bands),
        out_shape=jax.ShapeDtypeStruct(slab.shape, f32),
        in_specs=[hbm],
        out_specs=hbm,
        scratch_shapes=[pltpu.VMEM((bands, rows // bands, cols), f32), dma((bands,)), dma((bands,))],
        compiler_params=pltpu.CompilerParams(vmem_limit_bytes=57 * 2**20),
    )(mixed)


def solution(mesh):
    in_specs = (
        P("row", "col"),
        P("row", "col"),
        P("row", "col"),
        P(None, "row", None),
        P(None, "row", None),
    )
    out_specs = P("row", "col")
    return jax.shard_map(shards, mesh=mesh, in_specs=in_specs, out_specs=out_specs, check_vma=False)
```
